256 devices in a mesh: section: 16 (over x, y), dp: 16 (over z, core).
Axes of the slice: x: 4, y: 4, z: 8, core: 2. Of those that a mesh axis runs over, the one named last changes fastest.
Arguments:
- x_stash: bfloat16 [16, 6144, 768], P('section', 'dp'), may hold values from -6 to 6
- gain: float32 [16, 768], P('section'), may hold values from 0.5 to 1.5
- w_in: bfloat16 [16, 768, 3072], P('section'), may hold values from -0.21875 to 0.21875
- w_out: bfloat16 [16, 768, 3072], P('section'), may hold values from -0.0546875 to 0.0546875
- out_grad: bfloat16 [6144, 768], P('dp'), may hold values from -6 to 6
- lengths: int32 [16, 4], P('dp'), may hold values from 1 to 96, 288 in all within a row
- order: int32 [16, 4], P('dp'), may hold values from 0 to 3, each once within a row
Outputs:
- grad_input: bfloat16 [16, 6144, 768], P('section', 'dp')
- grad_w_in: float32 [16, 768, 3072], P('section', 'dp')
- grad_w_out: float32 [16, 768, 3072], P('section', 'dp')
The draws below stay inside these ranges and needn't reach their ends.
Inputs may be any that keep to these rules, and one draw needn't show every extreme that they name: The 4 lengths of each replica add up to 288, and the longest is exactly 96. `order`: each row names each of the 4 slots once.
All inputs are finite; a program needn't handle non-finite values.
Results may differ from the reference program's by a relative error of at most 0.035.
Values may be sent and summed in bfloat16 or wider, within the bound.
No kernel may reach another device: no remote copies, remote signals or barrier semaphores. Data moves between devices by JAX's collectives and lax.ppermute only.
A program may use at most 128 MiB of HBM per device.

```python
import math
from functools import partial
import jax
import jax.numpy as jnp
import numpy as np
from jax import lax

D = 768
H = 3072
MB = 4
TOK_MB = 96
TOKENS = 6144
N_SECTION = 16
N_DP = 16


def with_spikes(drawn, key, source, target, parts, factor):
    owner, partner = [(jnp.arange(drawn.shape[axis_at]) // (drawn.shape[axis_at] // parts)).reshape([-1 if axis == axis_at else 1 for axis in range(drawn.ndim)]) for axis_at in (source, target)]
    chosen = jax.random.permutation(key, parts)[partner]
    strong = (owner == chosen) | (owner == (partner + parts // 2) % parts)
    return jnp.where(strong, factor * drawn, drawn)


def shard_levels(own_key, dims, split, smallest, top_value):
    def one(axis_at, blocks):
        heights = jax.random.uniform(jax.random.fold_in(jax.random.fold_in(own_key, 6), axis_at), (blocks,), jnp.float32, smallest / len(split), top_value / len(split))
        return jnp.repeat(jnp.exp(heights), dims[axis_at] // blocks).reshape((-1,) + (1,) * (len(dims) - axis_at - 1))

    level = one(*split[0])
    for cut in split[1:]:
        level = level * one(*cut)
    return level


def profile(amount, total, limit, lean):
    loads = [(1 << 20) // math.isqrt(standing ** lean) + 1 for standing in range(2, amount + 1)]
    surplus, given = total - limit - (amount - 1), [1] * (amount - 1)
    while surplus > 0:
        candidates = [i for i in range(amount - 1) if given[i] < limit]
        pool, budget = sum([loads[i] for i in candidates]), surplus
        for i in candidates:
            more = min(limit - given[i], max(1, budget * loads[i] // pool), surplus)
            given[i] = given[i] + more
            surplus = surplus - more
    return np.array([limit] + given)


def ragged(key, amount, total, reach, lean):
    if amount == 2:
        one = jax.random.randint(key, (), max(1, total - reach), min(reach, total - 1) + 1)
        return jnp.stack([one, total - one])
    sizes = jnp.asarray(profile(amount, total, reach, lean), jnp.int32)
    pairs = (amount - 1) // 2
    donor, taker = sizes[1:1 + 2 * pairs:2], sizes[2:2 + 2 * pairs:2]
    slack = jnp.minimum(donor - 1, reach - taker)
    shifted = jax.random.randint(jax.random.fold_in(key, 1), (pairs,), 0, 1 << 20) % (slack + 1)
    sizes = sizes.at[1:1 + 2 * pairs:2].set(donor - shifted).at[2:2 + 2 * pairs:2].set(taker + shifted)
    return sizes[jax.random.permutation(jax.random.fold_in(key, 2), amount)]


def gaussian(own_key, shape, spread, most, split=(), kind=jnp.bfloat16):
    level = shard_levels(own_key, shape, split, -0.22, 0.18) if split else 1.0
    values = jax.random.normal(own_key, shape, jnp.float32) * spread * level
    return jnp.minimum(jnp.maximum(values, -most), most).astype(kind)


def gaussian_with(stream_key, extent, width, reach, cuts, heavy, kind=jnp.bfloat16):
    values = width * jax.random.normal(stream_key, extent, jnp.float32)
    if cuts:
        values = values * shard_levels(stream_key, extent, cuts, -0.22, 0.18)
    return jnp.clip(with_spikes(values, jax.random.fold_in(stream_key, 3), *heavy), -reach, reach).astype(kind)


def setup_inputs(seed: int = 0) -> dict:
    key_list = jax.random.split(jax.random.key(seed), 8)
    x_stash = gaussian(key_list[0], (N_SECTION, TOKENS, D), 1.0, 6.0, ((0, 16), (1, 16)))
    gain = jnp.clip(1.0 + 0.1 * jax.random.normal(key_list[1], (N_SECTION, D), jnp.float32), 0.5, 1.5)
    w_in = gaussian(key_list[2], (N_SECTION, D, H), D ** -0.5, 0.21875, ((0, 16),))
    w_out = gaussian(key_list[3], (N_SECTION, D, H), (D * N_SECTION) ** -0.5, 0.0546875, ((0, 16),))
    out_grad = gaussian_with(key_list[4], (TOKENS, D), 1.0, 6.0, ((0, 16),), (0, 1, 16, 2.0))
    lengths = jax.vmap(lambda own: ragged(own, MB, 3 * TOK_MB, TOK_MB, 2))(jax.random.split(key_list[5], N_DP)).reshape((N_DP, MB)).astype(jnp.int32)
    order = jax.vmap(lambda own: jax.random.permutation(own, MB))(jax.random.split(key_list[6], N_DP)).reshape((N_DP, MB)).astype(jnp.int32)
    return dict(x_stash=x_stash, gain=gain, w_in=w_in, w_out=w_out, out_grad=out_grad, lengths=lengths, order=order)


EPSILON = 1e-05

def transposed_dot(operand_a, operand_b):
    return lax.dot_general(operand_a, operand_b, (((0,), (0,)), ((), ())), preferred_element_type=jnp.float32)

def layer_backward(x_rows, dy_rows, gain_row, w_up, w_down):
    values = x_rows.astype(jnp.float32)
    centre = values - lax.optimization_barrier(jnp.mean(values, axis=1, keepdims=True))
    scale_inv = lax.rsqrt(lax.optimization_barrier(jnp.mean(centre * centre, axis=1, keepdims=True)) + EPSILON)
    normed = centre * scale_inv
    inputs = (normed * gain_row).astype(jnp.bfloat16)
    before = jnp.dot(inputs, w_up, preferred_element_type=jnp.float32)
    activated, pullback = jax.vjp(partial(jax.nn.gelu, approximate=True), before)
    hidden = activated.astype(jnp.bfloat16)
    d_hidden = jnp.dot(dy_rows, w_down, preferred_element_type=jnp.float32)
    d_before = pullback(d_hidden)[0].astype(jnp.bfloat16)
    d_inputs = lax.dot_general(d_before, w_up, (((1,), (1,)), ((), ())), preferred_element_type=jnp.float32)
    d_normed = d_inputs * gain_row
    correction = d_normed - lax.optimization_barrier(jnp.mean(d_normed, axis=1, keepdims=True)) - normed * lax.optimization_barrier(jnp.mean(d_normed * normed, axis=1, keepdims=True))
    d_rows = (dy_rows.astype(jnp.float32) + scale_inv * correction).astype(jnp.bfloat16)
    return (d_rows, inputs, d_before, hidden)

def reference(x_stash, gain, w_in, w_out, out_grad, lengths, order):
    slot_ids = jnp.arange(MB, dtype=jnp.int32)
    matches = order[:, :, None] == slot_ids[None, None, :]
    live_len = lax.optimization_barrier(jnp.sum(jnp.where(matches, lengths[:, :, None], 0), axis=1))
    positions = jnp.arange(TOK_MB, dtype=jnp.int32)
    keep_mask = (positions[None, None, :] < live_len[:, :, None]).reshape(TOKENS, 1)
    top_grad = jnp.where(keep_mask, out_grad, jnp.zeros_like(out_grad))

    def section_step(incoming, per_section):
        x_rows, gain_row, w_up, w_down = per_section
        d_rows, inputs, d_before, hidden = layer_backward(x_rows, incoming, gain_row, w_up, w_down)
        grad_up = transposed_dot(inputs, d_before) * (1.0 / N_DP)
        grad_down = transposed_dot(incoming, hidden) * (1.0 / N_DP)
        return (d_rows, (d_rows, grad_up, grad_down))
    _, outputs = lax.scan(section_step, top_grad, (x_stash, gain, w_in, w_out), reverse=True)
    return (outputs[0], outputs[1], outputs[2])
```

```python
from functools import partial

import jax
import jax.numpy as jnp
from jax import lax
from jax.experimental import pallas as pl
from jax.experimental.pallas import tpu as pltpu
from jax.sharding import PartitionSpec as P

LIVE = 288
CHUNKS = 3
EPSILON = 1e-05
GELU_C = 0.7978845608028654
GELU_K = 0.044715
F32 = jnp.float32
BF16 = jnp.bfloat16

VMEM = pl.BlockSpec(memory_space=pltpu.VMEM)
SMEM = pl.BlockSpec(memory_space=pltpu.SMEM)
HBM = pl.BlockSpec(memory_space=pltpu.HBM)
MIB = 1 << 20


def in_vmem(value):
    return pltpu.with_memory_space_constraint(value, pltpu.VMEM)


def vmem_array(shape, dtype):
    return pltpu.VMEM(shape, dtype)


def in_hbm(value):
    return pltpu.with_memory_space_constraint(value, pltpu.HBM)


def selector(len_ref, ord_ref, live, slots):
    count = len_ref.shape[1]
    width = slots // count
    p = lax.broadcasted_iota(jnp.int32, (live, slots), 0)
    q = lax.broadcasted_iota(jnp.int32, (live, slots), 1)
    target = jnp.full((live, slots), -1, jnp.int32)
    start = jnp.int32(0)
    for k in range(count):
        size = jnp.int32(0)
        for j in range(count):
            size = size + jnp.where(ord_ref[0, j] == k, len_ref[0, j], 0)
        inside = (q >= k * width) & (q < k * width + size)
        target = jnp.where(inside, q - k * width + start, target)
        start = start + size
    return (target == p).astype(F32).astype(BF16)


def prep_kernel(len_ref, ord_ref, x_ref, og_ref, gain_hbm, w_in_hbm, w_out_hbm,
                sel_ref, xhat_ref, rstd_ref, u_ref, hid_ref, gp_ref, top_ref, gain_ref, w_in_ref, w_out_ref, sems):
    copies = [
        pltpu.make_async_copy(source, target, sems.at[i])
        for i, (source, target) in enumerate(((gain_hbm, gain_ref), (w_in_hbm, w_in_ref), (w_out_hbm, w_out_ref)))
    ]
    for copy in copies:
        copy.start()
    live, slots = sel_ref.shape
    sel = selector(len_ref, ord_ref, live, slots)
    sel_ref[...] = sel
    top_ref[...] = jnp.dot(sel, og_ref[...], preferred_element_type=F32).astype(BF16)
    x = jnp.dot(sel, x_ref[...], preferred_element_type=F32)
    centre = x - jnp.mean(x, axis=1, keepdims=True)
    rstd = lax.rsqrt(jnp.mean(centre * centre, axis=1, keepdims=True) + EPSILON)
    xhat = centre * rstd
    xhat_ref[...] = xhat
    rstd_ref[...] = jnp.broadcast_to(rstd, rstd_ref.shape)
    copies[0].wait()
    u_ref[...] = (xhat * gain_ref[...]).astype(BF16)
    copies[1].wait()
    block = 512
    hidden = w_in_ref.shape[1]

    @pl.loop(0, hidden // block)
    def _(i):
        cols = pl.ds(pl.multiple_of(i * block, block), block)
        a = jnp.dot(u_ref[...], w_in_ref[:, cols], preferred_element_type=F32)
        t = jnp.tanh(GELU_C * (a + GELU_K * a * a * a))
        half = 0.5 * (1.0 + t)
        hid_ref[:, cols] = (a * half).astype(BF16)
        gp_ref[:, cols] = half + 0.5 * a * (1.0 - t * t) * (GELU_C * (1.0 + 3.0 * GELU_K * a * a))

    copies[2].wait()

def prep(lengths, order, x, out_grad, gain, w_in, w_out):
    slots, width = x.shape
    hidden = w_in.shape[1]
    live = LIVE * slots // 384
    return pl.pallas_call(
        prep_kernel,
        out_shape=(
            vmem_array((live, slots), BF16),
            vmem_array((live, width), F32),
            vmem_array((live, 128), F32),
            vmem_array((live, width), BF16),
            vmem_array((live, hidden), BF16),
            vmem_array((live, hidden), F32),
            vmem_array((live, width), BF16),
            vmem_array(gain.shape, F32),
            vmem_array(w_in.shape, BF16),
            vmem_array(w_out.shape, BF16),
        ),
        in_specs=[SMEM] * 2 + [VMEM] * 2 + [HBM] * 3,
        out_specs=(VMEM,) * 10,
        scratch_shapes=[pltpu.SemaphoreType.DMA((3,))],
        compiler_params=pltpu.CompilerParams(vmem_limit_bytes=16 * MIB),
        cost_estimate=pl.CostEstimate(
            flops=2 * live * width * hidden, bytes_accessed=4 * width * hidden, transcendentals=live * hidden),
        name="prep",
    )(lengths, order, in_vmem(x), in_vmem(out_grad), *(in_hbm(v) for v in (gain, w_in, w_out)))


def tick_kernel(ctl_ref, cur_ref, top_ref, xhat_ref, rstd_ref, gp_ref, gain_ref, w_in_ref, w_out_ref,
                da_in, dy_in, dx_in, out_ref, da_ref, dy_ref, dx_ref):
    del da_in, dy_in, dx_in
    rows_count = cur_ref.shape[0]

    @pl.when(ctl_ref[0] == 1)
    def _():
        rows = pl.ds(pl.multiple_of(ctl_ref[1] * rows_count, rows_count), rows_count)
        dy = jnp.where(ctl_ref[2] == 1, top_ref[rows, :], cur_ref[...])
        dy_ref[rows, :] = dy
        dh = jnp.dot(dy, w_out_ref[...], preferred_element_type=F32)
        da = (dh * gp_ref[rows, :]).astype(BF16)
        da_ref[rows, :] = da
        g = lax.dot_general(da, w_in_ref[...], (((1,), (1,)), ((), ())), preferred_element_type=F32)
        g = g * gain_ref[...]
        xhat = xhat_ref[rows, :]
        inner = g - jnp.mean(g, axis=1, keepdims=True) - xhat * jnp.mean(g * xhat, axis=1, keepdims=True)
        dx = (dy.astype(F32) + rstd_ref[rows, 0:1] * inner).astype(BF16)
        dx_ref[rows, :] = dx
        out_ref[...] = dx


def tick(ctl, cur, stage, stash):
    rows, width = cur.shape
    live, hidden = stash[0].shape
    big = tuple(in_vmem(v) for v in (cur,) + stage + stash)
    return pl.pallas_call(
        tick_kernel,
        out_shape=(
            vmem_array((rows, width), BF16),
            vmem_array((live, hidden), BF16),
            vmem_array((live, width), BF16),
            vmem_array((live, width), BF16),
        ),
        in_specs=[SMEM] + [VMEM] * 11,
        out_specs=(VMEM,) * 4,
        input_output_aliases={9: 1, 10: 2, 11: 3},
        compiler_params=pltpu.CompilerParams(vmem_limit_bytes=8 * MIB),
        cost_estimate=pl.CostEstimate(flops=4 * rows * width * hidden, bytes_accessed=4 * width * hidden, transcendentals=0),
        name="tick",
    )(ctl, *big)


def grads_kernel(u_ref, da_ref, dy_ref, hid_ref, out_ref, lhs):
    i = pl.program_id(0)
    half = pl.num_programs(0) // 2

    @pl.when(i == 0)
    def _():
        lhs[...] = u_ref[...].T

    @pl.when(i == half)
    def _():
        lhs[...] = dy_ref[...].T

    block = out_ref.shape[1]
    cols = pl.ds(pl.multiple_of(lax.rem(i, half) * block, block), block)

    @pl.when(i < half)
    def _():
        out_ref[...] = jnp.dot(lhs[...], da_ref[:, cols], preferred_element_type=F32).astype(BF16)

    @pl.when(i >= half)
    def _():
        out_ref[...] = jnp.dot(lhs[...], hid_ref[:, cols], preferred_element_type=F32).astype(BF16)


def grads(u, da, dy, hid):
    live, width = u.shape
    hidden = da.shape[1]
    block = 512
    return pl.pallas_call(
        grads_kernel,
        out_shape=jax.ShapeDtypeStruct((width, 2 * hidden), BF16),
        grid=(2 * hidden // block,),
        in_specs=[VMEM] * 4,
        out_specs=pl.BlockSpec((width, block), lambda i: (0, i)),
        scratch_shapes=[pltpu.VMEM((width, live), BF16)],
        compiler_params=pltpu.CompilerParams(vmem_limit_bytes=8 * MIB),
        cost_estimate=pl.CostEstimate(flops=4 * live * width * hidden, bytes_accessed=4 * width * hidden, transcendentals=0),
        name="weight_grads",
    )(*(in_vmem(v) for v in (u, da, dy, hid)))


def local(x_stash, gain, w_in, w_out, out_grad, lengths, order):
    sections = lax.axis_size("section")
    replicas = lax.axis_size("dp")
    me = lax.axis_index("section")
    slots, width = out_grad.shape
    hidden = w_in.shape[2]
    sel, xhat, rstd, u, hid, gp, top, gain_row, w_up, w_down = prep(
        lengths, order, x_stash[0], out_grad, gain, w_in[0], w_out[0])
    live = u.shape[0]
    rows = live // CHUNKS
    stage = (top, xhat, rstd, gp, gain_row, w_up, w_down)
    stash = (jnp.zeros((live, hidden), BF16), jnp.zeros((live, width), BF16), jnp.zeros((live, width), BF16))
    cur = jnp.zeros((rows, width), BF16)
    ticks = CHUNKS + sections - 1
    for t in range(ticks):
        chunk = t - (sections - 1 - me)
        active = (chunk >= 0) & (chunk < CHUNKS)
        ctl = jnp.stack([active.astype(jnp.int32), jnp.clip(chunk, 0, CHUNKS - 1), (me == sections - 1).astype(jnp.int32)])
        sent, *stash = tick(ctl, cur, stage, tuple(stash))
        pairs = [(s, s - 1) for s in range(1, sections) if 0 <= t - (sections - 1 - s) < CHUNKS]
        if pairs:
            cur = lax.ppermute(sent, "section", pairs)
    da, dy, dx = stash
    partial_sums = grads(u, da, dy, hid)
    grad_rows = lax.dot_general(sel, dx, (((0,), (0,)), ((), ())), preferred_element_type=F32).astype(BF16)
    summed = lax.psum_scatter(partial_sums, "dp", scatter_dimension=0, tiled=True).astype(F32) * (1.0 / replicas)
    return grad_rows[None], summed[:, :hidden][None], summed[:, hidden:][None]


def solution(mesh):
    return jax.shard_map(
        local,
        mesh=mesh,
        in_specs=(
            P("section", "dp", None),
            P("section", None),
            P("section", None, None),
            P("section", None, None),
            P("dp", None),
            P("dp", None),
            P("dp", None),
        ),
        out_specs=(P("section", "dp", None), P("section", "dp", None), P("section", "dp", None)),
        check_vma=False,
    )
```

```python
from functools import partial

import jax
import jax.numpy as jnp
from jax import lax
from jax.experimental import pallas as pl
from jax.experimental.pallas import tpu as pltpu
from jax.sharding import PartitionSpec as P

LIVE = 288
CHUNKS = 3
EPSILON = 1e-05
GELU_C = 0.7978845608028654
GELU_K = 0.044715
F32 = jnp.float32
BF16 = jnp.bfloat16

VMEM = pl.BlockSpec(memory_space=pltpu.VMEM)
SMEM = pl.BlockSpec(memory_space=pltpu.SMEM)
HBM = pl.BlockSpec(memory_space=pltpu.HBM)
MIB = 1 << 20


def in_vmem(value):
    return pltpu.with_memory_space_constraint(value, pltpu.VMEM)


def vmem_array(shape, dtype):
    return pltpu.VMEM(shape, dtype)


def in_hbm(value):
    return pltpu.with_memory_space_constraint(value, pltpu.HBM)


def selector(len_ref, ord_ref, live, slots):
    count = len_ref.shape[1]
    width = slots // count
    p = lax.broadcasted_iota(jnp.int32, (live, slots), 0)
    q = lax.broadcasted_iota(jnp.int32, (live, slots), 1)
    target = jnp.full((live, slots), -1, jnp.int32)
    start = jnp.int32(0)
    for k in range(count):
        size = jnp.int32(0)
        for j in range(count):
            size = size + jnp.where(ord_ref[0, j] == k, len_ref[0, j], 0)
        inside = (q >= k * width) & (q < k * width + size)
        target = jnp.where(inside, q - k * width + start, target)
        start = start + size
    return (target == p).astype(F32).astype(BF16)


def prep_kernel(len_ref, ord_ref, x_ref, og_ref, gain_hbm, w_in_hbm, w_out_hbm,
                sel_ref, xhat_ref, rstd_ref, u_ref, hid_ref, gp_ref, top_ref, gain_ref, w_in_t_ref, w_out_ref,
                da_ref, dy_ref, dx_ref, cur_ref, w_in_ref, sems):
    del da_ref, dy_ref, dx_ref, cur_ref
    copies = [
        pltpu.make_async_copy(source, target, sems.at[i])
        for i, (source, target) in enumerate(((gain_hbm, gain_ref), (w_in_hbm, w_in_ref), (w_out_hbm, w_out_ref)))
    ]
    for copy in copies:
        copy.start()
    live, slots = sel_ref.shape
    sel = selector(len_ref, ord_ref, live, slots)
    sel_ref[...] = sel
    top_ref[...] = jnp.dot(sel, og_ref[...], preferred_element_type=F32).astype(BF16)
    x = jnp.dot(sel, x_ref[...], preferred_element_type=F32)
    centre = x - jnp.mean(x, axis=1, keepdims=True)
    rstd = lax.rsqrt(jnp.mean(centre * centre, axis=1, keepdims=True) + EPSILON)
    xhat = centre * rstd
    xhat_ref[...] = xhat
    rstd_ref[...] = jnp.broadcast_to(rstd, rstd_ref.shape)
    copies[0].wait()
    u_ref[...] = (xhat * gain_ref[...]).astype(BF16)
    copies[1].wait()
    block = 512
    hidden = w_in_ref.shape[1]

    @pl.loop(0, hidden // block)
    def _(i):
        cols = pl.ds(pl.multiple_of(i * block, block), block)
        w = w_in_ref[:, cols]
        a = jnp.dot(u_ref[...], w, preferred_element_type=F32)
        w_in_t_ref[cols, :] = w.T
        t = jnp.tanh(GELU_C * (a + GELU_K * a * a * a))
        half = 0.5 * (1.0 + t)
        hid_ref[:, cols] = (a * half).astype(BF16)
        gp_ref[:, cols] = half + 0.5 * a * (1.0 - t * t) * (GELU_C * (1.0 + 3.0 * GELU_K * a * a))

    copies[2].wait()


def prep(lengths, order, x, out_grad, gain, w_in, w_out):
    slots, width = x.shape
    hidden = w_in.shape[1]
    live = LIVE * slots // 384
    return pl.pallas_call(
        prep_kernel,
        out_shape=(
            vmem_array((live, slots), BF16),
            vmem_array((live, width), F32),
            vmem_array((live, 128), F32),
            vmem_array((live, width), BF16),
            vmem_array((live, hidden), BF16),
            vmem_array((live, hidden), F32),
            vmem_array((live, width), BF16),
            vmem_array(gain.shape, F32),
            vmem_array((hidden, width), BF16),
            vmem_array(w_out.shape, BF16),
            vmem_array((live, hidden), BF16),
            vmem_array((live, width), BF16),
            vmem_array((live, width), BF16),
            vmem_array((live // CHUNKS, width), BF16),
        ),
        in_specs=[SMEM] * 2 + [VMEM] * 2 + [HBM] * 3,
        out_specs=(VMEM,) * 14,
        scratch_shapes=[pltpu.VMEM(w_in.shape, BF16), pltpu.SemaphoreType.DMA((3,))],
        compiler_params=pltpu.CompilerParams(vmem_limit_bytes=16 * MIB),
        cost_estimate=pl.CostEstimate(
            flops=2 * live * width * hidden, bytes_accessed=4 * width * hidden, transcendentals=live * hidden),
        name="prep",
    )(lengths, order, in_vmem(x), in_vmem(out_grad), *(in_hbm(v) for v in (gain, w_in, w_out)))


def tick_kernel(step, cur_ref, top_ref, xhat_ref, rstd_ref, gp_ref, gain_ref, w_in_t_ref, w_out_ref,
                da_in, dy_in, dx_in, out_ref, da_ref, dy_ref, dx_ref):
    del da_in, dy_in, dx_in
    rows_count = cur_ref.shape[0]
    hidden = w_in_t_ref.shape[0]
    width = w_out_ref.shape[0]
    last = lax.axis_size("section") - 1
    me = lax.axis_index("section")
    chunk = step - last + me
    block = 512

    @pl.when((chunk >= 0) & (chunk < CHUNKS))
    def _():
        rows = pl.ds(pl.multiple_of(chunk * rows_count, rows_count), rows_count)

        @pl.when(me == last)
        def _():
            dy_ref[rows, :] = top_ref[rows, :]

        @pl.when(me != last)
        def _():
            dy_ref[rows, :] = cur_ref[...]

        dy = dy_ref[rows, :]
        for i in range(hidden // block):
            cols = slice(i * block, (i + 1) * block)
            dh = jnp.dot(dy, w_out_ref[:, cols], preferred_element_type=F32)
            da_ref[rows, cols] = (dh * gp_ref[rows, cols]).astype(BF16)
        da = da_ref[rows, :]
        g = jnp.concatenate(
            [jnp.dot(da, w_in_t_ref[:, i:i + 256], preferred_element_type=F32) for i in range(0, width, 256)], axis=1)
        g = g * gain_ref[...]
        xhat = xhat_ref[rows, :]
        inner = g - jnp.mean(g, axis=1, keepdims=True) - xhat * jnp.mean(g * xhat, axis=1, keepdims=True)
        dx = (dy.astype(F32) + rstd_ref[rows, 0:1] * inner).astype(BF16)
        dx_ref[rows, :] = dx
        out_ref[...] = dx


def tick(step, cur, stage, stash):
    rows, width = cur.shape
    live, hidden = stash[0].shape
    big = tuple(in_vmem(v) for v in (cur,) + stage + stash)
    return pl.pallas_call(
        partial(tick_kernel, step),
        out_shape=(
            vmem_array((rows, width), BF16),
            vmem_array((live, hidden), BF16),
            vmem_array((live, width), BF16),
            vmem_array((live, width), BF16),
        ),
        in_specs=[VMEM] * 11,
        out_specs=(VMEM,) * 4,
        input_output_aliases={8: 1, 9: 2, 10: 3},
        compiler_params=pltpu.CompilerParams(vmem_limit_bytes=8 * MIB),
        cost_estimate=pl.CostEstimate(flops=4 * rows * width * hidden, bytes_accessed=4 * width * hidden, transcendentals=0),
        name="tick",
    )(*big)


def grads_kernel(u_ref, da_ref, dy_ref, hid_ref, out_ref):
    block = out_ref.shape[0]
    hidden = da_ref.shape[1]
    rows = pl.ds(pl.multiple_of(pl.program_id(0) * block, block), block)
    out_ref[:, :hidden] = jnp.dot(u_ref[:, rows].T, da_ref[...], preferred_element_type=F32).astype(BF16)
    out_ref[:, hidden:] = jnp.dot(dy_ref[:, rows].T, hid_ref[...], preferred_element_type=F32).astype(BF16)


def grads(u, da, dy, hid):
    live, width = u.shape
    hidden = da.shape[1]
    block = 256 if width % 256 == 0 else 128
    return pl.pallas_call(
        grads_kernel,
        out_shape=jax.ShapeDtypeStruct((width, 2 * hidden), BF16),
        grid=(width // block,),
        in_specs=[VMEM] * 4,
        out_specs=pl.BlockSpec((block, 2 * hidden), lambda i: (i, 0)),
        compiler_params=pltpu.CompilerParams(vmem_limit_bytes=20 * MIB),
        cost_estimate=pl.CostEstimate(flops=4 * live * width * hidden, bytes_accessed=4 * width * hidden, transcendentals=0),
        name="weight_grads",
    )(*(in_vmem(v) for v in (u, da, dy, hid)))


def unpack_kernel(sel_ref, dx_ref, out_ref):
    out_ref[...] = lax.dot_general(
        sel_ref[...], dx_ref[...], (((0,), (0,)), ((), ())), preferred_element_type=F32).astype(BF16)


def unpack(sel, dx):
    slots, width = sel.shape[1], dx.shape[1]
    return pl.pallas_call(
        unpack_kernel,
        out_shape=jax.ShapeDtypeStruct((slots, width), BF16),
        in_specs=[VMEM] * 2,
        out_specs=VMEM,
        compiler_params=pltpu.CompilerParams(vmem_limit_bytes=8 * MIB),
        cost_estimate=pl.CostEstimate(flops=2 * slots * width * dx.shape[0], bytes_accessed=4 * slots * width, transcendentals=0),
        name="unpack",
    )(in_vmem(sel), in_vmem(dx))


def local(x_stash, gain, w_in, w_out, out_grad, lengths, order):
    sections = lax.axis_size("section")
    replicas = lax.axis_size("dp")
    hidden = w_in.shape[2]
    sel, xhat, rstd, u, hid, gp, top, gain_row, w_up_t, w_down, da, dy, dx, cur = prep(
        lengths, order, x_stash[0], out_grad, gain, w_in[0], w_out[0])
    stage = (top, xhat, rstd, gp, gain_row, w_up_t, w_down)
    stash = (da, dy, dx)
    for t in range(CHUNKS + sections - 1):
        sent, *stash = tick(t, cur, stage, tuple(stash))
        pairs = [(s, s - 1) for s in range(1, sections) if 0 <= t - (sections - 1 - s) < CHUNKS]
        if pairs:
            cur = lax.ppermute(sent, "section", pairs)
    da, dy, dx = stash
    partial_sums = grads(u, da, dy, hid)
    grad_rows = unpack(sel, dx)
    summed = lax.psum_scatter(partial_sums, "dp", scatter_dimension=0, tiled=True).astype(F32) * (1.0 / replicas)
    return grad_rows[None], summed[:, :hidden][None], summed[:, hidden:][None]


def solution(mesh):
    return jax.shard_map(
        local,
        mesh=mesh,
        in_specs=(
            P("section", "dp", None),
            P("section", None),
            P("section", None, None),
            P("section", None, None),
            P("dp", None),
            P("dp", None),
            P("dp", None),
        ),
        out_specs=(P("section", "dp", None), P("section", "dp", None), P("section", "dp", None)),
        check_vma=False,
    )
```

```python
from functools import partial

import jax
import jax.numpy as jnp
from jax import lax
from jax.experimental import pallas as pl
from jax.experimental.pallas import tpu as pltpu
from jax.sharding import PartitionSpec as P

LIVE = 288
CHUNKS = 3
EPSILON = 1e-05
GELU_C = 0.7978845608028654
GELU_K = 0.044715
F32 = jnp.float32
BF16 = jnp.bfloat16

VMEM = pl.BlockSpec(memory_space=pltpu.VMEM)
SMEM = pl.BlockSpec(memory_space=pltpu.SMEM)
HBM = pl.BlockSpec(memory_space=pltpu.HBM)
MIB = 1 << 20


def in_vmem(value):
    return pltpu.with_memory_space_constraint(value, pltpu.VMEM)


def vmem_array(shape, dtype):
    return pltpu.VMEM(shape, dtype)


def in_hbm(value):
    return pltpu.with_memory_space_constraint(value, pltpu.HBM)


def selector(len_ref, ord_ref, live, slots):
    count = len_ref.shape[1]
    width = slots // count
    p = lax.broadcasted_iota(jnp.int32, (live, slots), 0)
    q = lax.broadcasted_iota(jnp.int32, (live, slots), 1)
    target = jnp.full((live, slots), -1, jnp.int32)
    start = jnp.int32(0)
    for k in range(count):
        size = jnp.int32(0)
        for j in range(count):
            size = size + jnp.where(ord_ref[0, j] == k, len_ref[0, j], 0)
        inside = (q >= k * width) & (q < k * width + size)
        target = jnp.where(inside, q - k * width + start, target)
        start = start + size
    return (target == p).astype(F32).astype(BF16)


def prep_kernel(len_ref, ord_ref, x_ref, og_ref, gain_hbm, w_in_hbm, w_out_hbm,
                sel_ref, xhat_ref, rstd_ref, u_ref, hid_ref, gp_ref, top_ref, gain_ref, w_in_t_ref, w_out_ref,
                da_ref, dy_ref, dx_ref, cur_ref, w_in_ref, sems):
    del da_ref, dy_ref, dx_ref, cur_ref
    copies = [
        pltpu.make_async_copy(source, target, sems.at[i])
        for i, (source, target) in enumerate(((gain_hbm, gain_ref), (w_in_hbm, w_in_ref), (w_out_hbm, w_out_ref)))
    ]
    for copy in copies:
        copy.start()
    live, slots = sel_ref.shape
    sel = selector(len_ref, ord_ref, live, slots)
    sel_ref[...] = sel
    top_ref[...] = jnp.dot(sel, og_ref[...], preferred_element_type=F32).astype(BF16)
    x = jnp.dot(sel, x_ref[...], preferred_element_type=F32)
    centre = x - jnp.mean(x, axis=1, keepdims=True)
    rstd = lax.rsqrt(jnp.mean(centre * centre, axis=1, keepdims=True) + EPSILON)
    xhat = centre * rstd
    xhat_ref[...] = xhat
    rstd_ref[...] = jnp.broadcast_to(rstd, rstd_ref.shape)
    copies[0].wait()
    u_ref[...] = (xhat * gain_ref[...]).astype(BF16)
    copies[1].wait()
    block = 512
    hidden = w_in_ref.shape[1]

    @pl.loop(0, hidden // block)
    def _(i):
        cols = pl.ds(pl.multiple_of(i * block, block), block)
        w = w_in_ref[:, cols]
        a = jnp.dot(u_ref[...], w, preferred_element_type=F32)
        w_in_t_ref[cols, :] = w.T
        t = jnp.tanh(GELU_C * (a + GELU_K * a * a * a))
        half = 0.5 * (1.0 + t)
        hid_ref[:, cols] = (a * half).astype(BF16)
        gp_ref[:, cols] = half + 0.5 * a * (1.0 - t * t) * (GELU_C * (1.0 + 3.0 * GELU_K * a * a))

    copies[2].wait()


def prep(lengths, order, x, out_grad, gain, w_in, w_out):
    slots, width = x.shape
    hidden = w_in.shape[1]
    live = LIVE * slots // 384
    return pl.pallas_call(
        prep_kernel,
        out_shape=(
            vmem_array((live, slots), BF16),
            vmem_array((live, width), F32),
            vmem_array((live, 128), F32),
            vmem_array((live, width), BF16),
            vmem_array((live, hidden), BF16),
            vmem_array((live, hidden), F32),
            vmem_array((live, width), BF16),
            vmem_array(gain.shape, F32),
            vmem_array((hidden, width), BF16),
            vmem_array(w_out.shape, BF16),
            vmem_array((live, hidden), BF16),
            vmem_array((live, width), BF16),
            vmem_array((live, width), BF16),
            vmem_array((live // CHUNKS, width), BF16),
        ),
        in_specs=[SMEM] * 2 + [VMEM] * 2 + [HBM] * 3,
        out_specs=(VMEM,) * 14,
        scratch_shapes=[pltpu.VMEM(w_in.shape, BF16), pltpu.SemaphoreType.DMA((3,))],
        compiler_params=pltpu.CompilerParams(vmem_limit_bytes=16 * MIB),
        cost_estimate=pl.CostEstimate(
            flops=2 * live * width * hidden, bytes_accessed=4 * width * hidden, transcendentals=live * hidden),
        name="prep",
    )(lengths, order, in_vmem(x), in_vmem(out_grad), *(in_hbm(v) for v in (gain, w_in, w_out)))


def tick_kernel(step, ship_rows, cur_ref, top_ref, xhat_ref, rstd_ref, gp_ref, gain_ref, w_in_t_ref, w_out_ref,
                u_ref, hid_ref, da_in, dy_in, dx_in, out_ref, da_ref, dy_ref, dx_ref, *ship):
    del da_in, dy_in, dx_in
    rows_count = cur_ref.shape[0]
    hidden = w_in_t_ref.shape[0]
    width = w_out_ref.shape[0]
    last = lax.axis_size("section") - 1
    me = lax.axis_index("section")
    chunk = step - last + me
    block = 512

    @pl.when((chunk >= 0) & (chunk < CHUNKS))
    def _():
        rows = pl.ds(pl.multiple_of(chunk * rows_count, rows_count), rows_count)

        @pl.when(me == last)
        def _():
            dy_ref[rows, :] = top_ref[rows, :]

        @pl.when(me != last)
        def _():
            dy_ref[rows, :] = cur_ref[...]

        dy = dy_ref[rows, :]
        for i in range(hidden // block):
            cols = slice(i * block, (i + 1) * block)
            dh = jnp.dot(dy, w_out_ref[:, cols], preferred_element_type=F32)
            da_ref[rows, cols] = (dh * gp_ref[rows, cols]).astype(BF16)
        da = da_ref[rows, :]
        g = jnp.concatenate(
            [jnp.dot(da, w_in_t_ref[:, i:i + 256], preferred_element_type=F32) for i in range(0, width, 256)], axis=1)
        g = g * gain_ref[...]
        xhat = xhat_ref[rows, :]
        inner = g - jnp.mean(g, axis=1, keepdims=True) - xhat * jnp.mean(g * xhat, axis=1, keepdims=True)
        dx = (dy.astype(F32) + rstd_ref[rows, 0:1] * inner).astype(BF16)
        dx_ref[rows, :] = dx
        out_ref[...] = dx

    if ship:
        first = lax.rem(lax.axis_index("dp"), 2) == 0
        part = slice(*ship_rows)

        @pl.when(first)
        def _():
            ship[0][:, :width] = dy_ref[part, :]
            ship[0][:, width:] = hid_ref[part, :]

        @pl.when(jnp.logical_not(first))
        def _():
            ship[0][:, :width] = u_ref[part, :]
            ship[0][:, width:] = da_ref[part, :]


def tick(step, cur, stage, stash, ship_rows=None):
    rows, width = cur.shape
    live, hidden = stash[0].shape
    big = tuple(in_vmem(v) for v in (cur,) + stage + stash)
    shapes = (
        vmem_array((rows, width), BF16),
        vmem_array((live, hidden), BF16),
        vmem_array((live, width), BF16),
        vmem_array((live, width), BF16),
    )
    if ship_rows:
        shapes += (vmem_array((ship_rows[1] - ship_rows[0], width + hidden), BF16),)
    return pl.pallas_call(
        partial(tick_kernel, step, ship_rows),
        out_shape=shapes,
        in_specs=[VMEM] * len(big),
        out_specs=(VMEM,) * len(shapes),
        input_output_aliases={10: 1, 11: 2, 12: 3},
        compiler_params=pltpu.CompilerParams(vmem_limit_bytes=8 * MIB),
        cost_estimate=pl.CostEstimate(flops=4 * rows * width * hidden, bytes_accessed=4 * width * hidden, transcendentals=0),
        name="tick",
    )(*big)


def ring_place(block):
    size = lax.axis_size("dp") // 2
    place = lax.axis_index("dp") // 2

    def rows(ahead, half):
        target = lax.rem(place + ahead + size, size)
        return pl.ds(pl.multiple_of(target * (2 * block) + half * block, 16), block)

    return rows


def first_kernel(far, u_ref, da_ref, dy_ref, hid_ref, got_a, got_b, lhs_ref, rhs_ref, right_ref, left_ref):
    live, width = u_ref.shape
    block = right_ref.shape[0]
    first = lax.rem(lax.axis_index("dp"), 2) == 0

    @pl.when(first)
    def _():
        lhs_ref[:, :live] = u_ref[...].T
        rhs_ref[:live, :] = da_ref[...]

    @pl.when(jnp.logical_not(first))
    def _():
        lhs_ref[:, :live] = dy_ref[...].T
        rhs_ref[:live, :] = hid_ref[...]

    at = live + got_a.shape[0]
    got = jnp.concatenate([got_a[:, :width], got_b[:, :width]], axis=0)
    lhs_ref[:, live:] = got.T
    rhs_ref[live:at, :] = got_a[:, width:]
    rhs_ref[at:, :] = got_b[:, width:]
    rows = ring_place(block)
    right_ref[...] = jnp.dot(lhs_ref[rows(far, 0), :], rhs_ref[...], preferred_element_type=F32).astype(BF16)
    left_ref[...] = jnp.dot(lhs_ref[rows(-far, 1), :], rhs_ref[...], preferred_element_type=F32).astype(BF16)


def second_kernel(far, lhs_ref, rhs_ref, all_ref, right_ref, left_ref):
    block = right_ref.shape[0]
    tile = 512
    hidden = rhs_ref.shape[1]
    for i in range(hidden // tile):
        cols = slice(i * tile, (i + 1) * tile)
        all_ref[:, cols] = jnp.dot(lhs_ref[...], rhs_ref[:, cols], preferred_element_type=F32).astype(BF16)
    rows = ring_place(block)
    right_ref[...] = all_ref[rows(far - 1, 1), :]
    left_ref[...] = all_ref[rows(1 - far, 0), :]


def hop_kernel(ahead, half, all_ref, from_left_ref, from_right_ref, right_ref, left_ref):
    rows = ring_place(right_ref.shape[0])
    right = from_left_ref[...].astype(F32) + all_ref[rows(ahead, half), :].astype(F32)
    right_ref[...] = right.astype(BF16)
    left = from_right_ref[...].astype(F32) + all_ref[rows(-ahead, 1 - half), :].astype(F32)
    left_ref[...] = left.astype(BF16)


def last_kernel(all_ref, right_0, left_1, right_1, left_0, keep_ref, send_ref):
    rows = ring_place(keep_ref.shape[0])
    first = lax.rem(lax.axis_index("dp"), 2) == 0
    half_0 = right_0[...].astype(F32) + left_0[...].astype(F32) + all_ref[rows(0, 0), :].astype(F32)
    half_1 = right_1[...].astype(F32) + left_1[...].astype(F32) + all_ref[rows(0, 1), :].astype(F32)
    scale = 1.0 / lax.axis_size("dp")
    keep_ref[...] = jnp.where(first, half_0, half_1) * scale
    send_ref[...] = jnp.where(first, half_1, half_0).astype(BF16)


def output_kernel(keep_ref, got_ref, in_ref, out_ref):
    first = lax.rem(lax.axis_index("dp"), 2) == 0
    got = got_ref[...].astype(F32) * (1.0 / lax.axis_size("dp"))
    keep = keep_ref[...]
    in_ref[...] = jnp.where(first, keep, got)
    out_ref[...] = jnp.where(first, got, keep)


def kernel_call(body, shapes, args, flops, name):
    return pl.pallas_call(
        body,
        out_shape=shapes,
        in_specs=[VMEM] * len(args),
        out_specs=(VMEM,) * len(shapes),
        compiler_params=pltpu.CompilerParams(vmem_limit_bytes=8 * MIB),
        cost_estimate=pl.CostEstimate(flops=flops, bytes_accessed=0, transcendentals=0),
        name=name,
    )(*(in_vmem(v) for v in args))


def reduce_grads(u, da, dy, hid, got_a, got_b):
    live, width = u.shape
    hidden = da.shape[1]
    count = lax.axis_size("dp")
    far = count // 4
    block = width // count
    piece = vmem_array((block, hidden), BF16)

    def around(value, chips):
        return lax.ppermute(value, "dp", [(i, (i + 2 * chips) % count) for i in range(count)])

    lhs, rhs, right, left = kernel_call(
        partial(first_kernel, far),
        (vmem_array((width, 2 * live), BF16), vmem_array((2 * live, hidden), BF16), piece, piece),
        (u, da, dy, hid, got_a, got_b), 8 * block * live * hidden, "first_blocks")
    even = around(right, 1), around(left, -1)
    total, right, left = kernel_call(
        partial(second_kernel, far), (vmem_array((width, hidden), BF16), piece, piece),
        (lhs, rhs), 4 * width * live * hidden, "all_blocks")
    odd = around(right, 1), around(left, -1)
    for ahead in range(far - 1, 0, -1):
        right, left = kernel_call(partial(hop_kernel, ahead, 0), (piece, piece), (total,) + even, 10 ** 9, "hop_even")
        even = around(right, 1), around(left, -1)
        if ahead > 1:
            right, left = kernel_call(partial(hop_kernel, ahead - 1, 1), (piece, piece), (total,) + odd, 10 ** 9, "hop_odd")
            odd = around(right, 1), around(left, -1)
    keep, send = kernel_call(
        last_kernel, (vmem_array((block, hidden), F32), piece), (total,) + even + odd, 10 ** 9, "last_sum")
    got = lax.ppermute(send, "dp", [(i, i ^ 1) for i in range(count)])
    return kernel_call(
        output_kernel, (jax.ShapeDtypeStruct((block, hidden), F32),) * 2, (keep, got), 10 ** 8, "outputs")


def unpack_kernel(sel_ref, dx_ref, out_ref):
    out_ref[...] = lax.dot_general(
        sel_ref[...], dx_ref[...], (((0,), (0,)), ((), ())), preferred_element_type=F32).astype(BF16)


def unpack(sel, dx):
    slots, width = sel.shape[1], dx.shape[1]
    return pl.pallas_call(
        unpack_kernel,
        out_shape=jax.ShapeDtypeStruct((slots, width), BF16),
        in_specs=[VMEM] * 2,
        out_specs=VMEM,
        compiler_params=pltpu.CompilerParams(vmem_limit_bytes=8 * MIB),
        cost_estimate=pl.CostEstimate(flops=2 * slots * width * dx.shape[0], bytes_accessed=4 * slots * width, transcendentals=0),
        name="unpack",
    )(in_vmem(sel), in_vmem(dx))


def local(x_stash, gain, w_in, w_out, out_grad, lengths, order):
    sections = lax.axis_size("section")
    replicas = lax.axis_size("dp")
    sel, xhat, rstd, u, hid, gp, top, gain_row, w_up_t, w_down, da, dy, dx, cur = prep(
        lengths, order, x_stash[0], out_grad, gain, w_in[0], w_out[0])
    stage = (top, xhat, rstd, gp, gain_row, w_up_t, w_down, u, hid)
    stash = (da, dy, dx)
    live, rows = u.shape[0], cur.shape[0]
    ticks = CHUNKS + sections - 1
    swap = [(i, i ^ 1) for i in range(replicas)]
    got = []
    for t in range(ticks):
        left = ticks - 1 - t
        ship_rows = {0: (live - rows, live), 1: (0, live - rows)}.get(left)
        sent, *stash = tick(t, cur, stage, tuple(stash), ship_rows)
        if ship_rows:
            got.append(lax.ppermute(stash.pop(), "dp", swap))
        pairs = [(s, s - 1) for s in range(1, sections) if 0 <= t - (sections - 1 - s) < CHUNKS]
        if pairs:
            cur = lax.ppermute(sent, "section", pairs)
    da, dy, dx = stash
    grad_in, grad_out = reduce_grads(u, da, dy, hid, *got)
    return unpack(sel, dx)[None], grad_in[None], grad_out[None]


def solution(mesh):
    return jax.shard_map(
        local,
        mesh=mesh,
        in_specs=(
            P("section", "dp", None),
            P("section", None),
            P("section", None, None),
            P("section", None, None),
            P("dp", None),
            P("dp", None),
            P("dp", None),
        ),
        out_specs=(P("section", "dp", None), P("section", "dp", None), P("section", "dp", None)),
        check_vma=False,
    )
```

```python
from functools import partial

import jax
import jax.numpy as jnp
from jax import lax
from jax.experimental import pallas as pl
from jax.experimental.pallas import tpu as pltpu
from jax.sharding import PartitionSpec as P

LIVE = 288
CHUNKS = 3
EPSILON = 1e-05
GELU_C = 0.7978845608028654
GELU_K = 0.044715
F32 = jnp.float32
BF16 = jnp.bfloat16

VMEM = pl.BlockSpec(memory_space=pltpu.VMEM)
HBM = pl.BlockSpec(memory_space=pltpu.HBM)
MIB = 1 << 20


def in_vmem(value):
    return pltpu.with_memory_space_constraint(value, pltpu.VMEM)


def vmem_array(shape, dtype):
    return pltpu.VMEM(shape, dtype)


def in_hbm(value):
    return pltpu.with_memory_space_constraint(value, pltpu.HBM)


def selector(len_ref, ord_ref, live, slots):
    count = len_ref.shape[1]
    width = slots // count
    p = lax.broadcasted_iota(jnp.int32, (live, slots), 0)
    q = lax.broadcasted_iota(jnp.int32, (live, slots), 1)
    target = jnp.full((live, slots), -1, jnp.int32)
    start = jnp.int32(0)
    for k in range(count):
        size = jnp.int32(0)
        for j in range(count):
            size = size + jnp.where(ord_ref[0, j] == k, len_ref[0, j], 0)
        inside = (q >= k * width) & (q < k * width + size)
        target = jnp.where(inside, q - k * width + start, target)
        start = start + size
    return (target == p).astype(F32).astype(BF16)


def gelu_rows(rows, cols, u_ref, w, hid_ref, gp_ref):
    a = jnp.dot(u_ref[rows, :], w, preferred_element_type=F32)
    square = a * a
    t = jnp.tanh(a * (GELU_C + (GELU_C * GELU_K) * square))
    half = 0.5 + 0.5 * t
    hid_ref[rows, cols] = (a * half).astype(BF16)
    slope = a * (0.5 * GELU_C + (1.5 * GELU_C * GELU_K) * square)
    gp_ref[rows, cols] = half + (1.0 - t * t) * slope


def prep_kernel(len_hbm, ord_hbm, x_hbm, og_hbm, gain_hbm, w_in_hbm, w_out_hbm,
                sel_ref, xhat_ref, rstd_ref, u_ref, hid_ref, gp_ref, top_ref, gain_ref, w_in_ref, w_in_t_ref, w_out_ref,
                da_ref, dy_ref, dx_ref, len_ref, ord_ref, x_ref, og_ref, sems):
    del da_ref, dy_ref, dx_ref
    pairs = ((len_hbm, len_ref), (ord_hbm, ord_ref), (x_hbm, x_ref), (og_hbm, og_ref), (gain_hbm, gain_ref),
             (w_in_hbm, w_in_ref), (w_out_hbm, w_out_ref))
    copies = [pltpu.make_async_copy(source, target, sems.at[i]) for i, (source, target) in enumerate(pairs)]
    for copy in copies:
        copy.start()
    live, slots = sel_ref.shape
    copies[0].wait()
    copies[1].wait()
    sel = selector(len_ref, ord_ref, live, slots)
    sel_ref[...] = sel
    copies[2].wait()
    x = jnp.dot(sel, x_ref[...], preferred_element_type=F32)
    centre = x - jnp.mean(x, axis=1, keepdims=True)
    rstd = lax.rsqrt(jnp.mean(centre * centre, axis=1, keepdims=True) + EPSILON)
    xhat = centre * rstd
    xhat_ref[...] = xhat
    rstd_ref[...] = jnp.broadcast_to(rstd, rstd_ref.shape)
    copies[3].wait()
    top_ref[...] = jnp.dot(sel, og_ref[...], preferred_element_type=F32).astype(BF16)
    copies[4].wait()
    u_ref[...] = (xhat * gain_ref[...]).astype(BF16)
    copies[5].wait()
    block = 512
    hidden = w_in_ref.shape[1]

    for i in range(hidden // block):
        cols = slice(i * block, (i + 1) * block)
        w = w_in_ref[:, cols]
        w_in_t_ref[cols, :] = w.T
        gelu_rows(slice(0, live // CHUNKS), cols, u_ref, w, hid_ref, gp_ref)

    copies[6].wait()


def prep(lengths, order, x, out_grad, gain, w_in, w_out):
    slots, width = x.shape
    hidden = w_in.shape[1]
    live = LIVE * slots // 384
    args = (lengths, order, x, out_grad, gain, w_in, w_out)
    return pl.pallas_call(
        prep_kernel,
        out_shape=(
            vmem_array((live, slots), BF16),
            vmem_array((live, width), F32),
            vmem_array((live, 128), F32),
            vmem_array((live, width), BF16),
            vmem_array((live, hidden), BF16),
            vmem_array((live, hidden), F32),
            vmem_array((live, width), BF16),
            vmem_array(gain.shape, F32),
            vmem_array(w_in.shape, BF16),
            vmem_array((hidden, width), BF16),
            vmem_array(w_out.shape, BF16),
            vmem_array((live, hidden), BF16),
            vmem_array((live, width), BF16),
            vmem_array((live, width), BF16),
        ),
        in_specs=[HBM] * len(args),
        out_specs=(VMEM,) * 14,
        scratch_shapes=[
            pltpu.SMEM(lengths.shape, jnp.int32),
            pltpu.SMEM(order.shape, jnp.int32),
            pltpu.VMEM(x.shape, BF16),
            pltpu.VMEM(out_grad.shape, BF16),
            pltpu.SemaphoreType.DMA((len(args),)),
        ],
        compiler_params=pltpu.CompilerParams(vmem_limit_bytes=16 * MIB),
        cost_estimate=pl.CostEstimate(
            flops=2 * live * width * hidden, bytes_accessed=4 * width * hidden, transcendentals=live * hidden),
        name="prep",
    )(*(in_hbm(v) for v in args))


def rest_kernel(u_ref, w_in_ref, hid_in, gp_in, hid_ref, gp_ref):
    del hid_in, gp_in
    live = u_ref.shape[0]
    block = 512
    hidden = w_in_ref.shape[1]

    for i in range(hidden // block):
        cols = slice(i * block, (i + 1) * block)
        gelu_rows(slice(live // CHUNKS, live), cols, u_ref, w_in_ref[:, cols], hid_ref, gp_ref)


def rest(u, w_in, hid, gp):
    args = tuple(in_vmem(v) for v in (u, w_in, hid, gp))
    return pl.pallas_call(
        rest_kernel,
        out_shape=(vmem_array(hid.shape, BF16), vmem_array(gp.shape, F32)),
        in_specs=[VMEM] * len(args),
        out_specs=(VMEM,) * 2,
        input_output_aliases={2: 0, 3: 1},
        compiler_params=pltpu.CompilerParams(vmem_limit_bytes=8 * MIB),
        cost_estimate=pl.CostEstimate(flops=2 * hid.size * u.shape[1], bytes_accessed=0, transcendentals=hid.size),
        name="rest",
    )(*args)


def tick_kernel(section, part, ship_rows, skip_dx, has_cur, *refs):
    cur_ref = refs[0] if has_cur else None
    (top_ref, xhat_ref, rstd_ref, gp_ref, gain_ref, w_in_t_ref, w_out_ref, u_ref, hid_ref,
     _, _, _, da_ref, dy_ref, dx_ref, *more) = refs[1:] if has_cur else refs
    hidden = w_in_t_ref.shape[0]
    width = w_out_ref.shape[0]
    rows = slice(*part)
    block = 512

    @pl.when(lax.axis_index("section") == section)
    def _():
        dy = cur_ref[...] if has_cur else top_ref[rows, :]
        dy_ref[rows, :] = dy
        for i in range(hidden // block):
            cols = slice(i * block, (i + 1) * block)
            dh = jnp.dot(dy, w_out_ref[:, cols], preferred_element_type=F32)
            da_ref[rows, cols] = (dh * gp_ref[rows, cols]).astype(BF16)
        if not skip_dx:
            dx = grad_rows_of(rows, dy, da_ref[rows, :], xhat_ref, rstd_ref, gain_ref, w_in_t_ref)
            dx_ref[rows, :] = dx
            if section:
                more[0][...] = dx

    if ship_rows:
        ship = more[-1]
        first = lax.rem(lax.axis_index("dp"), 2) == 0
        part = slice(*ship_rows)

        @pl.when(first)
        def _():
            ship[:, :width] = dy_ref[part, :]
            ship[:, width:] = hid_ref[part, :]

        @pl.when(jnp.logical_not(first))
        def _():
            ship[:, :width] = u_ref[part, :]
            ship[:, width:] = da_ref[part, :]


def tick(section, part, cur, stage, stash, ship_rows, skip_dx):
    live, hidden = stash[0].shape
    width = stash[1].shape[1]
    rows = part[1] - part[0]
    args = tuple(in_vmem(v) for v in (() if cur is None else (cur,)) + stage + stash)
    shapes = (
        vmem_array((live, hidden), BF16),
        vmem_array((live, width), BF16),
        vmem_array((live, width), BF16),
    )
    if section:
        shapes += (vmem_array((rows, width), BF16),)
    if ship_rows:
        shapes += (vmem_array((ship_rows[1] - ship_rows[0], width + hidden), BF16),)
    first = len(args) - len(stash)
    return pl.pallas_call(
        partial(tick_kernel, section, part, ship_rows, skip_dx, cur is not None),
        out_shape=shapes,
        in_specs=[VMEM] * len(args),
        out_specs=(VMEM,) * len(shapes),
        input_output_aliases={first + i: i for i in range(len(stash))},
        compiler_params=pltpu.CompilerParams(vmem_limit_bytes=8 * MIB),
        cost_estimate=pl.CostEstimate(
            flops=4 * rows * width * hidden if section else 10 ** 10, bytes_accessed=0, transcendentals=0),
        name="tick",
    )(*args)


def ring_place(block):
    size = lax.axis_size("dp") // 2
    place = lax.axis_index("dp") // 2

    def rows(ahead, half):
        target = lax.rem(place + ahead + size, size)
        return pl.ds(pl.multiple_of(target * (2 * block) + half * block, 16), block)

    return rows


def stage_kernel(far, u_ref, da_ref, dy_ref, hid_ref, got_ref, lhs_ref, rhs_ref, right_ref, left_ref):
    live, width = u_ref.shape
    block = right_ref.shape[0]
    first = lax.rem(lax.axis_index("dp"), 2) == 0
    ready = live + got_ref.shape[0]

    @pl.when(first)
    def _():
        lhs_ref[:, :live] = u_ref[...].T
        rhs_ref[:live, :] = da_ref[...]

    @pl.when(jnp.logical_not(first))
    def _():
        lhs_ref[:, :live] = dy_ref[...].T
        rhs_ref[:live, :] = hid_ref[...]

    lhs_ref[:, live:ready] = got_ref[:, :width].T
    rhs_ref[live:ready, :] = got_ref[:, width:]
    rows = ring_place(block)
    right_ref[...] = jnp.dot(lhs_ref[rows(far, 0), :ready], rhs_ref[:ready, :], preferred_element_type=F32)
    left_ref[...] = jnp.dot(lhs_ref[rows(-far, 1), :ready], rhs_ref[:ready, :], preferred_element_type=F32)


def first_kernel(far, right_part, left_part, got_ref, lhs_in, rhs_in, right_ref, left_ref, lhs_ref, rhs_ref):
    del lhs_in, rhs_in
    width, rows_all = lhs_ref.shape
    block = right_ref.shape[0]
    ready = rows_all - got_ref.shape[0]
    lhs_ref[:, ready:] = got_ref[:, :width].T
    rhs_ref[ready:, :] = got_ref[:, width:]
    rows = ring_place(block)
    right = jnp.dot(lhs_ref[rows(far, 0), ready:], rhs_ref[ready:, :], preferred_element_type=F32)
    right_ref[...] = (right_part[...] + right).astype(BF16)
    left = jnp.dot(lhs_ref[rows(-far, 1), ready:], rhs_ref[ready:, :], preferred_element_type=F32)
    left_ref[...] = (left_part[...] + left).astype(BF16)


def second_kernel(far, lhs_ref, rhs_ref, right_ref, left_ref):
    rows = ring_place(right_ref.shape[0])
    right_ref[...] = jnp.dot(lhs_ref[rows(far - 1, 1), :], rhs_ref[...], preferred_element_type=F32).astype(BF16)
    left_ref[...] = jnp.dot(lhs_ref[rows(1 - far, 0), :], rhs_ref[...], preferred_element_type=F32).astype(BF16)


def near_kernel(reach, lhs_ref, rhs_ref, _, all_ref, near_ref):
    block = all_ref.shape[0] // (2 * (2 * reach + 1))
    rows = ring_place(block)
    for k in range(-reach, reach + 1):
        for half in range(2):
            at = (2 * (k + reach) + half) * block
            near_ref[at:at + block, :] = lhs_ref[rows(k, half), :]
    tile = 512
    for i in range(rhs_ref.shape[1] // tile):
        cols = slice(i * tile, (i + 1) * tile)
        all_ref[:, cols] = jnp.dot(near_ref[...], rhs_ref[:, cols], preferred_element_type=F32).astype(BF16)


def near_rows(all_ref, block, ahead, half):
    reach = (all_ref.shape[0] // (2 * block) - 1) // 2
    at = (2 * (ahead + reach) + half) * block
    return all_ref[at:at + block, :].astype(F32)


def early_hop_kernel(ahead, lhs_ref, rhs_ref, from_left_ref, from_right_ref, right_ref, left_ref):
    rows = ring_place(right_ref.shape[0])
    right = jnp.dot(lhs_ref[rows(ahead, 0), :], rhs_ref[...], preferred_element_type=F32)
    right_ref[...] = (from_left_ref[...].astype(F32) + right).astype(BF16)
    left = jnp.dot(lhs_ref[rows(-ahead, 1), :], rhs_ref[...], preferred_element_type=F32)
    left_ref[...] = (from_right_ref[...].astype(F32) + left).astype(BF16)


def hop_kernel(ahead, half, all_ref, from_left_ref, from_right_ref, *refs):
    right_ref, left_ref = refs[-2:]
    block = right_ref.shape[0]
    right_ref[...] = (from_left_ref[...].astype(F32) + near_rows(all_ref, block, ahead, half)).astype(BF16)
    left_ref[...] = (from_right_ref[...].astype(F32) + near_rows(all_ref, block, -ahead, 1 - half)).astype(BF16)


def last_kernel(all_ref, right_0, left_1, right_1, left_0, keep_ref, send_ref):
    block = keep_ref.shape[0]
    first = lax.rem(lax.axis_index("dp"), 2) == 0
    half_0 = right_0[...].astype(F32) + left_0[...].astype(F32) + near_rows(all_ref, block, 0, 0)
    half_1 = right_1[...].astype(F32) + left_1[...].astype(F32) + near_rows(all_ref, block, 0, 1)
    scale = 1.0 / lax.axis_size("dp")
    keep_ref[...] = jnp.where(first, half_0, half_1) * scale
    send_ref[...] = jnp.where(first, half_1, half_0).astype(BF16)


def output_kernel(keep_ref, got_ref, in_ref, out_ref):
    first = lax.rem(lax.axis_index("dp"), 2) == 0
    got = got_ref[...].astype(F32) * (1.0 / lax.axis_size("dp"))
    keep = keep_ref[...]
    in_ref[...] = jnp.where(first, keep, got)
    out_ref[...] = jnp.where(first, got, keep)


def kernel_call(body, shapes, args, flops, name, aliases=None, gate=None, scratch=()):
    specs = [VMEM] * len(args)
    args = tuple(in_vmem(v) for v in args)
    if gate is not None:
        specs.append(HBM)
        args += (in_hbm(gate),)
    return pl.pallas_call(
        body,
        out_shape=shapes,
        in_specs=specs,
        out_specs=(VMEM,) * len(shapes),
        scratch_shapes=scratch,
        input_output_aliases=aliases or {},
        compiler_params=pltpu.CompilerParams(vmem_limit_bytes=8 * MIB),
        cost_estimate=pl.CostEstimate(flops=flops, bytes_accessed=0, transcendentals=0),
        name=name,
    )(*args)


def reduce_grads(u, da, dy, hid, got_a, got_b, gate):
    live, width = u.shape
    hidden = da.shape[1]
    count = lax.axis_size("dp")
    far = count // 4
    block = width // count
    piece = vmem_array((block, hidden), BF16)
    wide = vmem_array((block, hidden), F32)
    lhs_shape, rhs_shape = vmem_array((width, 2 * live), BF16), vmem_array((2 * live, hidden), BF16)
    small = 8 * block * live * hidden

    def around(value, chips):
        return lax.ppermute(value, "dp", [(i, (i + 2 * chips) % count) for i in range(count)])

    lhs, rhs, right, left = kernel_call(
        partial(stage_kernel, far), (lhs_shape, rhs_shape, wide, wide), (u, da, dy, hid, got_a), small, "stage")
    right, left, lhs, rhs = kernel_call(
        partial(first_kernel, far), (piece, piece, lhs_shape, rhs_shape), (right, left, got_b, lhs, rhs), small,
        "first_blocks", {3: 2, 4: 3})
    even = around(right, 1), around(left, -1)
    right, left = kernel_call(partial(second_kernel, far), (piece, piece), (lhs, rhs), small, "second_blocks")
    odd = around(right, 1), around(left, -1)
    right, left = kernel_call(
        partial(early_hop_kernel, far - 1), (piece, piece), (lhs, rhs) + even, small, "early_hop")
    even = around(right, 1), around(left, -1)
    near = (2 * far - 3) * 2 * block
    (total,) = kernel_call(
        partial(near_kernel, far - 2), (vmem_array((near, hidden), BF16),), (lhs, rhs, right),
        4 * near * live * hidden, "near_blocks", scratch=[pltpu.VMEM((near, 2 * live), BF16)])
    for ahead in range(far - 2, 0, -1):
        right, left = kernel_call(
            partial(hop_kernel, ahead, 1), (piece, piece), (total,) + odd, 10 ** 9, "hop_odd")
        odd = around(right, 1), around(left, -1)
        right, left = kernel_call(
            partial(hop_kernel, ahead, 0), (piece, piece), (total,) + even, 10 ** 9, "hop_even",
            gate=gate if ahead == 1 else None)
        even = around(right, 1), around(left, -1)
    keep, send = kernel_call(last_kernel, (wide, piece), (total,) + even + odd, 10 ** 9, "last_sum")
    got = lax.ppermute(send, "dp", [(i, i ^ 1) for i in range(count)])
    return kernel_call(
        output_kernel, (jax.ShapeDtypeStruct((block, hidden), F32),) * 2, (keep, got), 10 ** 8, "outputs")


def grad_rows_of(rows, dy, da, xhat_ref, rstd_ref, gain_ref, w_in_t_ref):
    g = jnp.concatenate(
        [jnp.dot(da, w_in_t_ref[:, i:i + 256], preferred_element_type=F32) for i in range(0, dy.shape[1], 256)], axis=1)
    g = g * gain_ref[...]
    xhat = xhat_ref[rows, :]
    inner = g - jnp.mean(g, axis=1, keepdims=True) - xhat * jnp.mean(g * xhat, axis=1, keepdims=True)
    return (dy.astype(F32) + rstd_ref[rows, 0:1] * inner).astype(BF16)


def unpack_kernel(part, sel_ref, dx_ref, dy_ref, da_ref, xhat_ref, rstd_ref, gain_ref, w_in_t_ref, out_ref, rows_ref):
    rows = slice(*part)
    rows_ref[...] = dx_ref[...]

    @pl.when(lax.axis_index("section") == 0)
    def _():
        rows_ref[rows, :] = grad_rows_of(rows, dy_ref[rows, :], da_ref[rows, :], xhat_ref, rstd_ref, gain_ref, w_in_t_ref)

    out_ref[...] = lax.dot_general(
        sel_ref[...], rows_ref[...], (((0,), (0,)), ((), ())), preferred_element_type=F32).astype(BF16)


def unpack(part, sel, dx, *rest_args):
    slots, width = sel.shape[1], dx.shape[1]
    args = tuple(in_vmem(v) for v in (sel, dx) + rest_args)
    return pl.pallas_call(
        partial(unpack_kernel, part),
        out_shape=jax.ShapeDtypeStruct((slots, width), BF16),
        in_specs=[VMEM] * len(args),
        out_specs=VMEM,
        scratch_shapes=[pltpu.VMEM(dx.shape, BF16)],
        compiler_params=pltpu.CompilerParams(vmem_limit_bytes=8 * MIB),
        cost_estimate=pl.CostEstimate(flops=2 * slots * width * dx.shape[0], bytes_accessed=0, transcendentals=0),
        name="unpack",
    )(*args)


def local(x_stash, gain, w_in, w_out, out_grad, lengths, order):
    sections = lax.axis_size("section")
    replicas = lax.axis_size("dp")
    sel, xhat, rstd, u, hid, gp, top, gain_row, w_up, w_up_t, w_down, *stash = prep(
        lengths, order, x_stash[0], out_grad, gain, w_in[0], w_out[0])
    rows = u.shape[0] // CHUNKS
    swap = [(i, i ^ 1) for i in range(replicas)]
    arrived, got = {}, []
    for t in range(CHUNKS + sections - 1):
        if t == 1:
            hid, gp = rest(u, w_up, hid, gp)
        stage = (top, xhat, rstd, gp, gain_row, w_up_t, w_down, u, hid)
        for chunk in reversed(range(CHUNKS)):
            section = sections - 1 - t + chunk
            if not 0 <= section < sections:
                continue
            ship_rows = None
            if section == 0 and chunk >= CHUNKS - 2:
                ship_rows = (0, chunk * rows + rows) if chunk == CHUNKS - 2 else (chunk * rows, chunk * rows + rows)
            part = (chunk * rows, chunk * rows + rows)
            skip_dx = section == 0 and chunk == CHUNKS - 1
            *stash, = tick(section, part, arrived.get(chunk), stage, tuple(stash), ship_rows, skip_dx)
            if ship_rows:
                got.append(lax.ppermute(stash.pop(), "dp", swap))
            if section:
                arrived[chunk] = lax.ppermute(stash.pop(), "section", [(section, section - 1)])
    da, dy, dx = stash
    grad_rows = unpack(part, sel, dx, dy, da, xhat, rstd, gain_row, w_up_t)
    grad_in, grad_out = reduce_grads(u, da, dy, hid, *got, grad_rows)
    return grad_rows[None], grad_in[None], grad_out[None]


def solution(mesh):
    return jax.shard_map(
        local,
        mesh=mesh,
        in_specs=(
            P("section", "dp", None),
            P("section", None),
            P("section", None, None),
            P("section", None, None),
            P("dp", None),
            P("dp", None),
            P("dp", None),
        ),
        out_specs=(P("section", "dp", None), P("section", "dp", None), P("section", "dp", None)),
        check_vma=False,
    )
```

```python
from functools import partial

import jax
import jax.numpy as jnp
from jax import lax
from jax.experimental import pallas as pl
from jax.experimental.pallas import tpu as pltpu
from jax.sharding import PartitionSpec as P

LIVE = 288
CHUNKS = 3
EPSILON = 1e-05
GELU_C = 0.7978845608028654
GELU_K = 0.044715
F32 = jnp.float32
BF16 = jnp.bfloat16

VMEM = pl.BlockSpec(memory_space=pltpu.VMEM)
HBM = pl.BlockSpec(memory_space=pltpu.HBM)
MIB = 1 << 20


def in_vmem(value):
    return pltpu.with_memory_space_constraint(value, pltpu.VMEM)


def vmem_array(shape, dtype):
    return pltpu.VMEM(shape, dtype)


def in_hbm(value):
    return pltpu.with_memory_space_constraint(value, pltpu.HBM)


def selector(len_ref, ord_ref, live, slots):
    count = len_ref.shape[1]
    width = slots // count
    p = lax.broadcasted_iota(jnp.int32, (live, slots), 0)
    q = lax.broadcasted_iota(jnp.int32, (live, slots), 1)
    target = jnp.full((live, slots), -1, jnp.int32)
    start = jnp.int32(0)
    for k in range(count):
        size = jnp.int32(0)
        for j in range(count):
            size = size + jnp.where(ord_ref[0, j] == k, len_ref[0, j], 0)
        inside = (q >= k * width) & (q < k * width + size)
        target = jnp.where(inside, q - k * width + start, target)
        start = start + size
    return (target == p).astype(F32).astype(BF16)


def gelu_rows(rows, cols, u_ref, w, hid_ref, gp_ref):
    a = jnp.dot(u_ref[rows, :], w, preferred_element_type=F32)
    square = a * a
    t = jnp.tanh(a * (GELU_C + (GELU_C * GELU_K) * square))
    half = 0.5 + 0.5 * t
    hid_ref[rows, cols] = (a * half).astype(BF16)
    slope = a * (0.5 * GELU_C + (1.5 * GELU_C * GELU_K) * square)
    gp_ref[rows, cols] = half + (1.0 - t * t) * slope


def prep_kernel(len_hbm, ord_hbm, x_hbm, og_hbm, gain_hbm, w_in_hbm, w_out_hbm,
                sel_ref, xhat_ref, rstd_ref, u_ref, hid_ref, gp_ref, top_ref, gain_ref, w_in_ref, w_in_t_ref, w_out_ref,
                da_ref, dy_ref, dx_ref, len_ref, ord_ref, x_ref, og_ref, sems):
    del da_ref, dy_ref, dx_ref
    block = 512
    blocks = [slice(i, i + block) for i in range(0, w_in_ref.shape[1], block)]
    pairs = [(len_hbm, len_ref), (ord_hbm, ord_ref), (x_hbm, x_ref), (gain_hbm, gain_ref)]
    pairs += [(w_in_hbm.at[:, cols], w_in_ref.at[:, cols]) for cols in blocks]
    pairs += [(og_hbm, og_ref), (w_out_hbm, w_out_ref)]
    copies = [pltpu.make_async_copy(source, target, sems.at[i]) for i, (source, target) in enumerate(pairs)]
    for copy in copies:
        copy.start()
    live, slots = sel_ref.shape
    copies[0].wait()
    copies[1].wait()
    sel = selector(len_ref, ord_ref, live, slots)
    sel_ref[...] = sel
    copies[2].wait()
    x = jnp.dot(sel, x_ref[...], preferred_element_type=F32)
    centre = x - jnp.mean(x, axis=1, keepdims=True)
    rstd = lax.rsqrt(jnp.mean(centre * centre, axis=1, keepdims=True) + EPSILON)
    xhat = centre * rstd
    xhat_ref[...] = xhat
    rstd_ref[...] = jnp.broadcast_to(rstd, rstd_ref.shape)
    copies[3].wait()
    u_ref[...] = (xhat * gain_ref[...]).astype(BF16)
    for copy, cols in zip(copies[4:-2], blocks):
        copy.wait()
        w = w_in_ref[:, cols]
        w_in_t_ref[cols, :] = w.T
        gelu_rows(slice(0, live // CHUNKS), cols, u_ref, w, hid_ref, gp_ref)
    copies[-2].wait()
    top_ref[...] = jnp.dot(sel, og_ref[...], preferred_element_type=F32).astype(BF16)
    copies[-1].wait()


def prep(lengths, order, x, out_grad, gain, w_in, w_out):
    slots, width = x.shape
    hidden = w_in.shape[1]
    live = LIVE * slots // 384
    args = (lengths, order, x, out_grad, gain, w_in, w_out)
    return pl.pallas_call(
        prep_kernel,
        out_shape=(
            vmem_array((live, slots), BF16),
            vmem_array((live, width), F32),
            vmem_array((live, 128), F32),
            vmem_array((live, width), BF16),
            vmem_array((live, hidden), BF16),
            vmem_array((live, hidden), F32),
            vmem_array((live, width), BF16),
            vmem_array(gain.shape, F32),
            vmem_array(w_in.shape, BF16),
            vmem_array((hidden, width), BF16),
            vmem_array(w_out.shape, BF16),
            vmem_array((live, hidden), BF16),
            vmem_array((live, width), BF16),
            vmem_array((live, width), BF16),
        ),
        in_specs=[HBM] * len(args),
        out_specs=(VMEM,) * 14,
        scratch_shapes=[
            pltpu.SMEM(lengths.shape, jnp.int32),
            pltpu.SMEM(order.shape, jnp.int32),
            pltpu.VMEM(x.shape, BF16),
            pltpu.VMEM(out_grad.shape, BF16),
            pltpu.SemaphoreType.DMA((len(args) - 1 + hidden // 512,)),
        ],
        compiler_params=pltpu.CompilerParams(vmem_limit_bytes=16 * MIB),
        cost_estimate=pl.CostEstimate(
            flops=2 * live * width * hidden, bytes_accessed=4 * width * hidden, transcendentals=live * hidden),
        name="prep",
    )(*(in_hbm(v) for v in args))


def rest_kernel(u_ref, w_in_ref, hid_in, gp_in, hid_ref, gp_ref):
    del hid_in, gp_in
    live = u_ref.shape[0]
    block = 512
    hidden = w_in_ref.shape[1]

    for i in range(hidden // block):
        cols = slice(i * block, (i + 1) * block)
        gelu_rows(slice(live // CHUNKS, live), cols, u_ref, w_in_ref[:, cols], hid_ref, gp_ref)


def rest(u, w_in, hid, gp):
    args = tuple(in_vmem(v) for v in (u, w_in, hid, gp))
    return pl.pallas_call(
        rest_kernel,
        out_shape=(vmem_array(hid.shape, BF16), vmem_array(gp.shape, F32)),
        in_specs=[VMEM] * len(args),
        out_specs=(VMEM,) * 2,
        input_output_aliases={2: 0, 3: 1},
        compiler_params=pltpu.CompilerParams(vmem_limit_bytes=8 * MIB),
        cost_estimate=pl.CostEstimate(flops=2 * hid.size * u.shape[1], bytes_accessed=0, transcendentals=hid.size),
        name="rest",
    )(*args)


def tick_kernel(section, part, ship_rows, skip_dx, has_cur, *refs):
    cur_ref = refs[0] if has_cur else None
    (top_ref, xhat_ref, rstd_ref, gp_ref, gain_ref, w_in_t_ref, w_out_ref, u_ref, hid_ref,
     _, _, _, da_ref, dy_ref, dx_ref, *more) = refs[1:] if has_cur else refs
    hidden = w_in_t_ref.shape[0]
    width = w_out_ref.shape[0]
    rows = slice(*part)
    block = 512

    @pl.when(lax.axis_index("section") == section)
    def _():
        dy = cur_ref[...] if has_cur else top_ref[rows, :]
        dy_ref[rows, :] = dy
        for i in range(hidden // block):
            cols = slice(i * block, (i + 1) * block)
            dh = jnp.dot(dy, w_out_ref[:, cols], preferred_element_type=F32)
            da_ref[rows, cols] = (dh * gp_ref[rows, cols]).astype(BF16)
        if not skip_dx:
            dx = grad_rows_of(rows, dy, da_ref[rows, :], xhat_ref, rstd_ref, gain_ref, w_in_t_ref)
            dx_ref[rows, :] = dx
            if section:
                more[0][...] = dx

    if ship_rows:
        ship = more[-1]
        first = lax.rem(lax.axis_index("dp"), 2) == 0
        part = slice(*ship_rows)

        @pl.when(first)
        def _():
            ship[:, :width] = dy_ref[part, :]
            ship[:, width:] = hid_ref[part, :]

        @pl.when(jnp.logical_not(first))
        def _():
            ship[:, :width] = u_ref[part, :]
            ship[:, width:] = da_ref[part, :]


def tick(section, part, cur, stage, stash, ship_rows, skip_dx):
    live, hidden = stash[0].shape
    width = stash[1].shape[1]
    rows = part[1] - part[0]
    args = tuple(in_vmem(v) for v in (() if cur is None else (cur,)) + stage + stash)
    shapes = (
        vmem_array((live, hidden), BF16),
        vmem_array((live, width), BF16),
        vmem_array((live, width), BF16),
    )
    if section:
        shapes += (vmem_array((rows, width), BF16),)
    if ship_rows:
        shapes += (vmem_array((ship_rows[1] - ship_rows[0], width + hidden), BF16),)
    first = len(args) - len(stash)
    return pl.pallas_call(
        partial(tick_kernel, section, part, ship_rows, skip_dx, cur is not None),
        out_shape=shapes,
        in_specs=[VMEM] * len(args),
        out_specs=(VMEM,) * len(shapes),
        input_output_aliases={first + i: i for i in range(len(stash))},
        compiler_params=pltpu.CompilerParams(vmem_limit_bytes=8 * MIB),
        cost_estimate=pl.CostEstimate(
            flops=4 * rows * width * hidden if section else 10 ** 10, bytes_accessed=0, transcendentals=0),
        name="tick",
    )(*args)


def ring_place(block):
    size = lax.axis_size("dp") // 2
    place = lax.axis_index("dp") // 2

    def rows(ahead, half):
        target = lax.rem(place + ahead + size, size)
        return pl.ds(pl.multiple_of(target * (2 * block) + half * block, 16), block)

    return rows


def stage_kernel(far, u_ref, da_ref, dy_ref, hid_ref, got_ref, lhs_ref, rhs_ref, right_ref, left_ref):
    live, width = u_ref.shape
    block = right_ref.shape[0]
    first = lax.rem(lax.axis_index("dp"), 2) == 0
    ready = live + got_ref.shape[0]

    @pl.when(first)
    def _():
        lhs_ref[:, :live] = u_ref[...].T
        rhs_ref[:live, :] = da_ref[...]

    @pl.when(jnp.logical_not(first))
    def _():
        lhs_ref[:, :live] = dy_ref[...].T
        rhs_ref[:live, :] = hid_ref[...]

    lhs_ref[:, live:ready] = got_ref[:, :width].T
    rhs_ref[live:ready, :] = got_ref[:, width:]
    rows = ring_place(block)
    right_ref[...] = jnp.dot(lhs_ref[rows(far, 0), :ready], rhs_ref[:ready, :], preferred_element_type=F32)
    left_ref[...] = jnp.dot(lhs_ref[rows(-far, 1), :ready], rhs_ref[:ready, :], preferred_element_type=F32)


def first_kernel(far, right_part, left_part, got_ref, lhs_in, rhs_in, right_ref, left_ref, lhs_ref, rhs_ref):
    del lhs_in, rhs_in
    width, rows_all = lhs_ref.shape
    block = right_ref.shape[0]
    ready = rows_all - got_ref.shape[0]
    lhs_ref[:, ready:] = got_ref[:, :width].T
    rhs_ref[ready:, :] = got_ref[:, width:]
    rows = ring_place(block)
    right = jnp.dot(lhs_ref[rows(far, 0), ready:], rhs_ref[ready:, :], preferred_element_type=F32)
    right_ref[...] = (right_part[...] + right).astype(BF16)
    left = jnp.dot(lhs_ref[rows(-far, 1), ready:], rhs_ref[ready:, :], preferred_element_type=F32)
    left_ref[...] = (left_part[...] + left).astype(BF16)


def second_kernel(far, lhs_ref, rhs_ref, right_ref, left_ref, next_right_ref, next_left_ref):
    rows = ring_place(right_ref.shape[0])
    right_ref[...] = jnp.dot(lhs_ref[rows(far - 1, 1), :], rhs_ref[...], preferred_element_type=F32).astype(BF16)
    left_ref[...] = jnp.dot(lhs_ref[rows(1 - far, 0), :], rhs_ref[...], preferred_element_type=F32).astype(BF16)
    next_right_ref[...] = jnp.dot(lhs_ref[rows(far - 1, 0), :], rhs_ref[...], preferred_element_type=F32)
    next_left_ref[...] = jnp.dot(lhs_ref[rows(1 - far, 1), :], rhs_ref[...], preferred_element_type=F32)


def near_kernel(reach, lhs_ref, rhs_ref, _, all_ref, near_ref):
    block = all_ref.shape[0] // (2 * (2 * reach + 1))
    rows = ring_place(block)
    for k in range(-reach, reach + 1):
        for half in range(2):
            at = (2 * (k + reach) + half) * block
            near_ref[at:at + block, :] = lhs_ref[rows(k, half), :]
    tile = 512
    for i in range(rhs_ref.shape[1] // tile):
        cols = slice(i * tile, (i + 1) * tile)
        all_ref[:, cols] = jnp.dot(near_ref[...], rhs_ref[:, cols], preferred_element_type=F32).astype(BF16)


def near_rows(all_ref, block, ahead, half):
    reach = (all_ref.shape[0] // (2 * block) - 1) // 2
    at = (2 * (ahead + reach) + half) * block
    return all_ref[at:at + block, :].astype(F32)


def early_hop_kernel(own_right_ref, own_left_ref, from_left_ref, from_right_ref, right_ref, left_ref):
    right_ref[...] = (from_left_ref[...].astype(F32) + own_right_ref[...]).astype(BF16)
    left_ref[...] = (from_right_ref[...].astype(F32) + own_left_ref[...]).astype(BF16)


def hop_kernel(ahead, half, all_ref, from_left_ref, from_right_ref, *refs):
    right_ref, left_ref = refs[-2:]
    block = right_ref.shape[0]
    right_ref[...] = (from_left_ref[...].astype(F32) + near_rows(all_ref, block, ahead, half)).astype(BF16)
    left_ref[...] = (from_right_ref[...].astype(F32) + near_rows(all_ref, block, -ahead, 1 - half)).astype(BF16)


def last_kernel(all_ref, right_0, left_1, right_1, left_0, keep_ref, send_ref):
    block = keep_ref.shape[0]
    first = lax.rem(lax.axis_index("dp"), 2) == 0
    half_0 = right_0[...].astype(F32) + left_0[...].astype(F32) + near_rows(all_ref, block, 0, 0)
    half_1 = right_1[...].astype(F32) + left_1[...].astype(F32) + near_rows(all_ref, block, 0, 1)
    scale = 1.0 / lax.axis_size("dp")
    keep_ref[...] = jnp.where(first, half_0, half_1) * scale
    send_ref[...] = jnp.where(first, half_1, half_0).astype(BF16)


def output_kernel(keep_ref, got_ref, in_ref, out_ref):
    first = lax.rem(lax.axis_index("dp"), 2) == 0
    got = got_ref[...].astype(F32) * (1.0 / lax.axis_size("dp"))
    keep = keep_ref[...]
    in_ref[...] = jnp.where(first, keep, got)
    out_ref[...] = jnp.where(first, got, keep)


def kernel_call(body, shapes, args, flops, name, aliases=None, gate=None, scratch=()):
    specs = [VMEM] * len(args)
    args = tuple(in_vmem(v) for v in args)
    if gate is not None:
        specs.append(HBM)
        args += (in_hbm(gate),)
    return pl.pallas_call(
        body,
        out_shape=shapes,
        in_specs=specs,
        out_specs=(VMEM,) * len(shapes),
        scratch_shapes=scratch,
        input_output_aliases=aliases or {},
        compiler_params=pltpu.CompilerParams(vmem_limit_bytes=8 * MIB),
        cost_estimate=pl.CostEstimate(flops=flops, bytes_accessed=0, transcendentals=0),
        name=name,
    )(*args)


def reduce_grads(u, da, dy, hid, got_a, got_b, gate):
    live, width = u.shape
    hidden = da.shape[1]
    count = lax.axis_size("dp")
    far = count // 4
    block = width // count
    piece = vmem_array((block, hidden), BF16)
    wide = vmem_array((block, hidden), F32)
    lhs_shape, rhs_shape = vmem_array((width, 2 * live), BF16), vmem_array((2 * live, hidden), BF16)
    small = 8 * block * live * hidden

    def around(value, chips):
        return lax.ppermute(value, "dp", [(i, (i + 2 * chips) % count) for i in range(count)])

    lhs, rhs, right, left = kernel_call(
        partial(stage_kernel, far), (lhs_shape, rhs_shape, wide, wide), (u, da, dy, hid, got_a), small, "stage")
    right, left, lhs, rhs = kernel_call(
        partial(first_kernel, far), (piece, piece, lhs_shape, rhs_shape), (right, left, got_b, lhs, rhs), small,
        "first_blocks", {3: 2, 4: 3})
    even = around(right, 1), around(left, -1)
    right, left, *own = kernel_call(
        partial(second_kernel, far), (piece, piece, wide, wide), (lhs, rhs), small, "second_blocks")
    odd = around(right, 1), around(left, -1)
    right, left = kernel_call(early_hop_kernel, (piece, piece), (*own, *even), 10 ** 9, "early_hop")
    even = around(right, 1), around(left, -1)
    near = (2 * far - 3) * 2 * block
    (total,) = kernel_call(
        partial(near_kernel, far - 2), (vmem_array((near, hidden), BF16),), (lhs, rhs, right),
        4 * near * live * hidden, "near_blocks", scratch=[pltpu.VMEM((near, 2 * live), BF16)])
    for ahead in range(far - 2, 0, -1):
        right, left = kernel_call(
            partial(hop_kernel, ahead, 1), (piece, piece), (total,) + odd, 10 ** 9, "hop_odd")
        odd = around(right, 1), around(left, -1)
        right, left = kernel_call(
            partial(hop_kernel, ahead, 0), (piece, piece), (total,) + even, 10 ** 9, "hop_even",
            gate=gate if ahead == 1 else None)
        even = around(right, 1), around(left, -1)
    keep, send = kernel_call(last_kernel, (wide, piece), (total,) + even + odd, 10 ** 9, "last_sum")
    got = lax.ppermute(send, "dp", [(i, i ^ 1) for i in range(count)])
    return kernel_call(
        output_kernel, (jax.ShapeDtypeStruct((block, hidden), F32),) * 2, (keep, got), 10 ** 8, "outputs")


def grad_rows_of(rows, dy, da, xhat_ref, rstd_ref, gain_ref, w_in_t_ref):
    g = jnp.concatenate(
        [jnp.dot(da, w_in_t_ref[:, i:i + 256], preferred_element_type=F32) for i in range(0, dy.shape[1], 256)], axis=1)
    g = g * gain_ref[...]
    xhat = xhat_ref[rows, :]
    inner = g - jnp.mean(g, axis=1, keepdims=True) - xhat * jnp.mean(g * xhat, axis=1, keepdims=True)
    return (dy.astype(F32) + rstd_ref[rows, 0:1] * inner).astype(BF16)


def unpack_kernel(part, sel_ref, dx_ref, dy_ref, da_ref, xhat_ref, rstd_ref, gain_ref, w_in_t_ref, out_ref, rows_ref):
    rows = slice(*part)
    rows_ref[...] = dx_ref[...]

    @pl.when(lax.axis_index("section") == 0)
    def _():
        rows_ref[rows, :] = grad_rows_of(rows, dy_ref[rows, :], da_ref[rows, :], xhat_ref, rstd_ref, gain_ref, w_in_t_ref)

    out_ref[...] = lax.dot_general(
        sel_ref[...], rows_ref[...], (((0,), (0,)), ((), ())), preferred_element_type=F32).astype(BF16)


def unpack(part, sel, dx, *rest_args):
    slots, width = sel.shape[1], dx.shape[1]
    args = tuple(in_vmem(v) for v in (sel, dx) + rest_args)
    return pl.pallas_call(
        partial(unpack_kernel, part),
        out_shape=jax.ShapeDtypeStruct((slots, width), BF16),
        in_specs=[VMEM] * len(args),
        out_specs=VMEM,
        scratch_shapes=[pltpu.VMEM(dx.shape, BF16)],
        compiler_params=pltpu.CompilerParams(vmem_limit_bytes=8 * MIB),
        cost_estimate=pl.CostEstimate(flops=2 * slots * width * dx.shape[0], bytes_accessed=0, transcendentals=0),
        name="unpack",
    )(*args)


def local(x_stash, gain, w_in, w_out, out_grad, lengths, order):
    sections = lax.axis_size("section")
    replicas = lax.axis_size("dp")
    sel, xhat, rstd, u, hid, gp, top, gain_row, w_up, w_up_t, w_down, *stash = prep(
        lengths, order, x_stash[0], out_grad, gain, w_in[0], w_out[0])
    rows = u.shape[0] // CHUNKS
    swap = [(i, i ^ 1) for i in range(replicas)]
    arrived, got = {}, []
    for t in range(CHUNKS + sections - 1):
        if t == 1:
            hid, gp = rest(u, w_up, hid, gp)
        stage = (top, xhat, rstd, gp, gain_row, w_up_t, w_down, u, hid)
        for chunk in reversed(range(CHUNKS)):
            section = sections - 1 - t + chunk
            if not 0 <= section < sections:
                continue
            ship_rows = None
            if section == 0 and chunk >= CHUNKS - 2:
                ship_rows = (0, chunk * rows + rows) if chunk == CHUNKS - 2 else (chunk * rows, chunk * rows + rows)
            part = (chunk * rows, chunk * rows + rows)
            skip_dx = section == 0 and chunk == CHUNKS - 1
            *stash, = tick(section, part, arrived.get(chunk), stage, tuple(stash), ship_rows, skip_dx)
            if ship_rows:
                got.append(lax.ppermute(stash.pop(), "dp", swap))
            if section:
                arrived[chunk] = lax.ppermute(stash.pop(), "section", [(section, section - 1)])
    da, dy, dx = stash
    grad_rows = unpack(part, sel, dx, dy, da, xhat, rstd, gain_row, w_up_t)
    grad_in, grad_out = reduce_grads(u, da, dy, hid, *got, grad_rows)
    return grad_rows[None], grad_in[None], grad_out[None]


def solution(mesh):
    return jax.shard_map(
        local,
        mesh=mesh,
        in_specs=(
            P("section", "dp", None),
            P("section", None),
            P("section", None, None),
            P("section", None, None),
            P("dp", None),
            P("dp", None),
            P("dp", None),
        ),
        out_specs=(P("section", "dp", None), P("section", "dp", None), P("section", "dp", None)),
        check_vma=False,
    )
```

```python
from functools import partial

import jax
import jax.numpy as jnp
from jax import lax
from jax.experimental import pallas as pl
from jax.experimental.pallas import tpu as pltpu
from jax.sharding import PartitionSpec as P

LIVE = 288
CHUNKS = 3
EPSILON = 1e-05
GELU_C = 0.7978845608028654
GELU_K = 0.044715
F32 = jnp.float32
BF16 = jnp.bfloat16

VMEM = pl.BlockSpec(memory_space=pltpu.VMEM)
HBM = pl.BlockSpec(memory_space=pltpu.HBM)
MIB = 1 << 20


def in_vmem(value):
    return pltpu.with_memory_space_constraint(value, pltpu.VMEM)


def vmem_array(shape, dtype):
    return pltpu.VMEM(shape, dtype)


def in_hbm(value):
    return pltpu.with_memory_space_constraint(value, pltpu.HBM)


def selector(len_ref, ord_ref, live, slots):
    count = len_ref.shape[1]
    width = slots // count
    p = lax.broadcasted_iota(jnp.int32, (live, slots), 0)
    q = lax.broadcasted_iota(jnp.int32, (live, slots), 1)
    target = jnp.full((live, slots), -1, jnp.int32)
    start = jnp.int32(0)
    for k in range(count):
        size = jnp.int32(0)
        for j in range(count):
            size = size + jnp.where(ord_ref[0, j] == k, len_ref[0, j], 0)
        inside = (q >= k * width) & (q < k * width + size)
        target = jnp.where(inside, q - k * width + start, target)
        start = start + size
    return (target == p).astype(F32).astype(BF16)


def gelu_rows(rows, cols, u_ref, w, hid_ref, gp_ref):
    a = jnp.dot(u_ref[rows, :], w, preferred_element_type=F32)
    square = a * a
    t = jnp.tanh(a * (GELU_C + (GELU_C * GELU_K) * square))
    half = 0.5 + 0.5 * t
    hid_ref[rows, cols] = (a * half).astype(BF16)
    slope = a * (0.5 * GELU_C + (1.5 * GELU_C * GELU_K) * square)
    gp_ref[rows, cols] = half + (1.0 - t * t) * slope


def prep_kernel(len_hbm, ord_hbm, x_hbm, og_hbm, gain_hbm, w_in_hbm, w_out_hbm,
                sel_ref, xhat_ref, rstd_ref, u_ref, hid_ref, gp_ref, top_ref, gain_ref, w_in_ref, w_in_t_ref, w_out_ref,
                da_ref, dy_ref, dx_ref, len_ref, ord_ref, x_ref, og_ref, sems):
    del da_ref, dy_ref, dx_ref
    block = 512
    blocks = [slice(i, i + block) for i in range(0, w_in_ref.shape[1], block)]
    pairs = [(len_hbm, len_ref), (ord_hbm, ord_ref), (x_hbm, x_ref), (gain_hbm, gain_ref)]
    pairs += [(w_in_hbm.at[:, cols], w_in_ref.at[:, cols]) for cols in blocks]
    pairs += [(og_hbm, og_ref), (w_out_hbm, w_out_ref)]
    copies = [pltpu.make_async_copy(source, target, sems.at[i]) for i, (source, target) in enumerate(pairs)]
    for copy in copies:
        copy.start()
    live, slots = sel_ref.shape
    copies[0].wait()
    copies[1].wait()
    sel = selector(len_ref, ord_ref, live, slots)
    sel_ref[...] = sel
    copies[2].wait()
    x = jnp.dot(sel, x_ref[...], preferred_element_type=F32)
    centre = x - jnp.mean(x, axis=1, keepdims=True)
    rstd = lax.rsqrt(jnp.mean(centre * centre, axis=1, keepdims=True) + EPSILON)
    xhat = centre * rstd
    xhat_ref[...] = xhat
    rstd_ref[...] = jnp.broadcast_to(rstd, rstd_ref.shape)
    copies[3].wait()
    u_ref[...] = (xhat * gain_ref[...]).astype(BF16)
    for copy, cols in zip(copies[4:-2], blocks):
        copy.wait()
        w = w_in_ref[:, cols]
        w_in_t_ref[cols, :] = w.T
        gelu_rows(slice(0, live // CHUNKS), cols, u_ref, w, hid_ref, gp_ref)
    copies[-2].wait()
    top_ref[...] = jnp.dot(sel, og_ref[...], preferred_element_type=F32).astype(BF16)
    copies[-1].wait()


def prep(lengths, order, x, out_grad, gain, w_in, w_out):
    slots, width = x.shape
    hidden = w_in.shape[1]
    live = LIVE * slots // 384
    args = (lengths, order, x, out_grad, gain, w_in, w_out)
    return pl.pallas_call(
        prep_kernel,
        out_shape=(
            vmem_array((live, slots), BF16),
            vmem_array((live, width), F32),
            vmem_array((live, 128), F32),
            vmem_array((live, width), BF16),
            vmem_array((live, hidden), BF16),
            vmem_array((live, hidden), F32),
            vmem_array((live, width), BF16),
            vmem_array(gain.shape, F32),
            vmem_array(w_in.shape, BF16),
            vmem_array((hidden, width), BF16),
            vmem_array(w_out.shape, BF16),
            vmem_array((live, hidden), BF16),
            vmem_array((live, width), BF16),
            vmem_array((live, width), BF16),
        ),
        in_specs=[HBM] * len(args),
        out_specs=(VMEM,) * 14,
        scratch_shapes=[
            pltpu.SMEM(lengths.shape, jnp.int32),
            pltpu.SMEM(order.shape, jnp.int32),
            pltpu.VMEM(x.shape, BF16),
            pltpu.VMEM(out_grad.shape, BF16),
            pltpu.SemaphoreType.DMA((len(args) - 1 + hidden // 512,)),
        ],
        compiler_params=pltpu.CompilerParams(vmem_limit_bytes=16 * MIB),
        cost_estimate=pl.CostEstimate(
            flops=2 * live * width * hidden, bytes_accessed=4 * width * hidden, transcendentals=live * hidden),
        name="prep",
    )(*(in_hbm(v) for v in args))


def rest_kernel(u_ref, w_in_ref, hid_in, gp_in, hid_ref, gp_ref):
    del hid_in, gp_in
    live = u_ref.shape[0]
    block = 512
    hidden = w_in_ref.shape[1]

    for i in range(hidden // block):
        cols = slice(i * block, (i + 1) * block)
        gelu_rows(slice(live // CHUNKS, live), cols, u_ref, w_in_ref[:, cols], hid_ref, gp_ref)


def rest(u, w_in, hid, gp):
    args = tuple(in_vmem(v) for v in (u, w_in, hid, gp))
    return pl.pallas_call(
        rest_kernel,
        out_shape=(vmem_array(hid.shape, BF16), vmem_array(gp.shape, F32)),
        in_specs=[VMEM] * len(args),
        out_specs=(VMEM,) * 2,
        input_output_aliases={2: 0, 3: 1},
        compiler_params=pltpu.CompilerParams(vmem_limit_bytes=8 * MIB),
        cost_estimate=pl.CostEstimate(flops=2 * hid.size * u.shape[1], bytes_accessed=0, transcendentals=hid.size),
        name="rest",
    )(*args)


def tick_kernel(section, part, ship_rows, skip_dx, has_cur, *refs):
    cur_ref = refs[0] if has_cur else None
    (top_ref, xhat_ref, rstd_ref, gp_ref, gain_ref, w_in_t_ref, w_out_ref, u_ref, hid_ref,
     _, _, _, da_ref, dy_ref, dx_ref, *more) = refs[1:] if has_cur else refs
    hidden = w_in_t_ref.shape[0]
    width = w_out_ref.shape[0]
    rows = slice(*part)
    block = 512

    @pl.when(lax.axis_index("section") == section)
    def _():
        dy = cur_ref[...] if has_cur else top_ref[rows, :]
        dy_ref[rows, :] = dy
        for i in range(hidden // block):
            cols = slice(i * block, (i + 1) * block)
            dh = jnp.dot(dy, w_out_ref[:, cols], preferred_element_type=F32)
            da_ref[rows, cols] = (dh * gp_ref[rows, cols]).astype(BF16)
        if not skip_dx:
            dx = grad_rows_of(rows, dy, da_ref[rows, :], xhat_ref, rstd_ref, gain_ref, w_in_t_ref)
            dx_ref[rows, :] = dx
            if section:
                more[0][...] = dx

    if ship_rows:
        ship = more[-1]
        first = lax.rem(lax.axis_index("dp"), 2) == 0
        part = slice(*ship_rows)

        @pl.when(first)
        def _():
            ship[:, :width] = dy_ref[part, :]
            ship[:, width:] = hid_ref[part, :]

        @pl.when(jnp.logical_not(first))
        def _():
            ship[:, :width] = u_ref[part, :]
            ship[:, width:] = da_ref[part, :]


def tick(section, part, cur, stage, stash, ship_rows, skip_dx):
    live, hidden = stash[0].shape
    width = stash[1].shape[1]
    rows = part[1] - part[0]
    args = tuple(in_vmem(v) for v in (() if cur is None else (cur,)) + stage + stash)
    shapes = (
        vmem_array((live, hidden), BF16),
        vmem_array((live, width), BF16),
        vmem_array((live, width), BF16),
    )
    if section:
        shapes += (vmem_array((rows, width), BF16),)
    if ship_rows:
        shapes += (vmem_array((ship_rows[1] - ship_rows[0], width + hidden), BF16),)
    first = len(args) - len(stash)
    return pl.pallas_call(
        partial(tick_kernel, section, part, ship_rows, skip_dx, cur is not None),
        out_shape=shapes,
        in_specs=[VMEM] * len(args),
        out_specs=(VMEM,) * len(shapes),
        input_output_aliases={first + i: i for i in range(len(stash))},
        compiler_params=pltpu.CompilerParams(vmem_limit_bytes=8 * MIB),
        cost_estimate=pl.CostEstimate(
            flops=10 ** 10 if skip_dx else 4 * rows * width * hidden, bytes_accessed=0, transcendentals=0),
        name="tick",
    )(*args)


def ring_place(block):
    size = lax.axis_size("dp") // 2
    place = lax.axis_index("dp") // 2

    def rows(ahead, half):
        target = lax.rem(place + ahead + size, size)
        return pl.ds(pl.multiple_of(target * (2 * block) + half * block, 16), block)

    return rows


def stage_kernel(far, u_ref, da_ref, dy_ref, hid_ref, got_ref, lhs_ref, rhs_ref, right_ref, left_ref):
    live, width = u_ref.shape
    block = right_ref.shape[0]
    first = lax.rem(lax.axis_index("dp"), 2) == 0
    ready = live + got_ref.shape[0]

    @pl.when(first)
    def _():
        lhs_ref[:, :live] = u_ref[...].T
        rhs_ref[:live, :] = da_ref[...]

    @pl.when(jnp.logical_not(first))
    def _():
        lhs_ref[:, :live] = dy_ref[...].T
        rhs_ref[:live, :] = hid_ref[...]

    lhs_ref[:, live:ready] = got_ref[:, :width].T
    rhs_ref[live:ready, :] = got_ref[:, width:]
    rows = ring_place(block)
    right_ref[...] = jnp.dot(lhs_ref[rows(far, 0), :ready], rhs_ref[:ready, :], preferred_element_type=F32)
    left_ref[...] = jnp.dot(lhs_ref[rows(-far, 1), :ready], rhs_ref[:ready, :], preferred_element_type=F32)


def first_kernel(far, right_part, left_part, got_ref, lhs_in, rhs_in, right_ref, left_ref, lhs_ref, rhs_ref):
    del lhs_in, rhs_in
    width, rows_all = lhs_ref.shape
    block = right_ref.shape[0]
    ready = rows_all - got_ref.shape[0]
    lhs_ref[:, ready:] = got_ref[:, :width].T
    rhs_ref[ready:, :] = got_ref[:, width:]
    rows = ring_place(block)
    right = jnp.dot(lhs_ref[rows(far, 0), ready:], rhs_ref[ready:, :], preferred_element_type=F32)
    right_ref[...] = (right_part[...] + right).astype(BF16)
    left = jnp.dot(lhs_ref[rows(-far, 1), ready:], rhs_ref[ready:, :], preferred_element_type=F32)
    left_ref[...] = (left_part[...] + left).astype(BF16)


def second_kernel(far, lhs_ref, rhs_ref, right_ref, left_ref, next_right_ref, next_left_ref):
    rows = ring_place(right_ref.shape[0])
    right_ref[...] = jnp.dot(lhs_ref[rows(far - 1, 1), :], rhs_ref[...], preferred_element_type=F32).astype(BF16)
    left_ref[...] = jnp.dot(lhs_ref[rows(1 - far, 0), :], rhs_ref[...], preferred_element_type=F32).astype(BF16)
    next_right_ref[...] = jnp.dot(lhs_ref[rows(far - 1, 0), :], rhs_ref[...], preferred_element_type=F32)
    next_left_ref[...] = jnp.dot(lhs_ref[rows(1 - far, 1), :], rhs_ref[...], preferred_element_type=F32)


def near_kernel(reach, lhs_ref, rhs_ref, _, all_ref, near_ref):
    block = all_ref.shape[0] // (2 * (2 * reach + 1))
    rows = ring_place(block)
    for k in range(-reach, reach + 1):
        for half in range(2):
            at = (2 * (k + reach) + half) * block
            near_ref[at:at + block, :] = lhs_ref[rows(k, half), :]
    tile = 512
    for i in range(rhs_ref.shape[1] // tile):
        cols = slice(i * tile, (i + 1) * tile)
        all_ref[:, cols] = jnp.dot(near_ref[...], rhs_ref[:, cols], preferred_element_type=F32).astype(BF16)


def near_rows(all_ref, block, ahead, half):
    reach = (all_ref.shape[0] // (2 * block) - 1) // 2
    at = (2 * (ahead + reach) + half) * block
    return all_ref[at:at + block, :].astype(F32)


def early_hop_kernel(own_right_ref, own_left_ref, from_left_ref, from_right_ref, right_ref, left_ref):
    right_ref[...] = (from_left_ref[...].astype(F32) + own_right_ref[...]).astype(BF16)
    left_ref[...] = (from_right_ref[...].astype(F32) + own_left_ref[...]).astype(BF16)


def hop_kernel(ahead, half, all_ref, from_left_ref, from_right_ref, *refs):
    right_ref, left_ref = refs[-2:]
    block = right_ref.shape[0]
    right_ref[...] = (from_left_ref[...].astype(F32) + near_rows(all_ref, block, ahead, half)).astype(BF16)
    left_ref[...] = (from_right_ref[...].astype(F32) + near_rows(all_ref, block, -ahead, 1 - half)).astype(BF16)


def last_kernel(all_ref, right_0, left_1, right_1, left_0, keep_ref, send_ref):
    block = keep_ref.shape[0]
    first = lax.rem(lax.axis_index("dp"), 2) == 0
    half_0 = right_0[...].astype(F32) + left_0[...].astype(F32) + near_rows(all_ref, block, 0, 0)
    half_1 = right_1[...].astype(F32) + left_1[...].astype(F32) + near_rows(all_ref, block, 0, 1)
    scale = 1.0 / lax.axis_size("dp")
    keep_ref[...] = jnp.where(first, half_0, half_1) * scale
    send_ref[...] = jnp.where(first, half_1, half_0).astype(BF16)


def output_kernel(keep_ref, got_ref, in_ref, out_ref):
    first = lax.rem(lax.axis_index("dp"), 2) == 0
    got = got_ref[...].astype(F32) * (1.0 / lax.axis_size("dp"))
    keep = keep_ref[...]
    in_ref[...] = jnp.where(first, keep, got)
    out_ref[...] = jnp.where(first, got, keep)


def kernel_call(body, shapes, args, flops, name, aliases=None, gate=None, scratch=()):
    specs = [VMEM] * len(args)
    args = tuple(in_vmem(v) for v in args)
    if gate is not None:
        specs.append(HBM)
        args += (in_hbm(gate),)
    return pl.pallas_call(
        body,
        out_shape=shapes,
        in_specs=specs,
        out_specs=(VMEM,) * len(shapes),
        scratch_shapes=scratch,
        input_output_aliases=aliases or {},
        compiler_params=pltpu.CompilerParams(vmem_limit_bytes=8 * MIB),
        cost_estimate=pl.CostEstimate(flops=flops, bytes_accessed=0, transcendentals=0),
        name=name,
    )(*args)


def reduce_grads(u, da, dy, hid, got_a, got_b, gate):
    live, width = u.shape
    hidden = da.shape[1]
    count = lax.axis_size("dp")
    far = count // 4
    block = width // count
    piece = vmem_array((block, hidden), BF16)
    wide = vmem_array((block, hidden), F32)
    lhs_shape, rhs_shape = vmem_array((width, 2 * live), BF16), vmem_array((2 * live, hidden), BF16)
    small = 8 * block * live * hidden

    def around(value, chips):
        return lax.ppermute(value, "dp", [(i, (i + 2 * chips) % count) for i in range(count)])

    lhs, rhs, right, left = kernel_call(
        partial(stage_kernel, far), (lhs_shape, rhs_shape, wide, wide), (u, da, dy, hid, got_a), small, "stage")
    right, left, lhs, rhs = kernel_call(
        partial(first_kernel, far), (piece, piece, lhs_shape, rhs_shape), (right, left, got_b, lhs, rhs), small,
        "first_blocks", {3: 2, 4: 3})
    even = around(right, 1), around(left, -1)
    right, left, *own = kernel_call(
        partial(second_kernel, far), (piece, piece, wide, wide), (lhs, rhs), small, "second_blocks")
    odd = around(right, 1), around(left, -1)
    right, left = kernel_call(early_hop_kernel, (piece, piece), (*own, *even), 10 ** 9, "early_hop")
    even = around(right, 1), around(left, -1)
    near = (2 * far - 3) * 2 * block
    (total,) = kernel_call(
        partial(near_kernel, far - 2), (vmem_array((near, hidden), BF16),), (lhs, rhs, right),
        4 * near * live * hidden, "near_blocks", scratch=[pltpu.VMEM((near, 2 * live), BF16)])
    for ahead in range(far - 2, 0, -1):
        right, left = kernel_call(
            partial(hop_kernel, ahead, 1), (piece, piece), (total,) + odd, 10 ** 9, "hop_odd")
        odd = around(right, 1), around(left, -1)
        right, left = kernel_call(
            partial(hop_kernel, ahead, 0), (piece, piece), (total,) + even, 10 ** 9, "hop_even",
            gate=gate if ahead == 1 else None)
        even = around(right, 1), around(left, -1)
    keep, send = kernel_call(last_kernel, (wide, piece), (total,) + even + odd, 10 ** 9, "last_sum")
    got = lax.ppermute(send, "dp", [(i, i ^ 1) for i in range(count)])
    return kernel_call(
        output_kernel, (jax.ShapeDtypeStruct((block, hidden), F32),) * 2, (keep, got), 10 ** 8, "outputs")


def grad_rows_of(rows, dy, da, xhat_ref, rstd_ref, gain_ref, w_in_t_ref):
    g = jnp.concatenate(
        [jnp.dot(da, w_in_t_ref[:, i:i + 256], preferred_element_type=F32) for i in range(0, dy.shape[1], 256)], axis=1)
    g = g * gain_ref[...]
    xhat = xhat_ref[rows, :]
    inner = g - jnp.mean(g, axis=1, keepdims=True) - xhat * jnp.mean(g * xhat, axis=1, keepdims=True)
    return (dy.astype(F32) + rstd_ref[rows, 0:1] * inner).astype(BF16)


def unpack_kernel(part, sel_ref, dx_ref, dy_ref, da_ref, xhat_ref, rstd_ref, gain_ref, w_in_t_ref, out_ref, rows_ref):
    rows = slice(*part)
    rows_ref[...] = dx_ref[...]

    @pl.when(lax.axis_index("section") == 0)
    def _():
        rows_ref[rows, :] = grad_rows_of(rows, dy_ref[rows, :], da_ref[rows, :], xhat_ref, rstd_ref, gain_ref, w_in_t_ref)

    out_ref[...] = lax.dot_general(
        sel_ref[...], rows_ref[...], (((0,), (0,)), ((), ())), preferred_element_type=F32).astype(BF16)


def unpack(part, sel, dx, *rest_args):
    slots, width = sel.shape[1], dx.shape[1]
    args = tuple(in_vmem(v) for v in (sel, dx) + rest_args)
    return pl.pallas_call(
        partial(unpack_kernel, part),
        out_shape=jax.ShapeDtypeStruct((slots, width), BF16),
        in_specs=[VMEM] * len(args),
        out_specs=VMEM,
        scratch_shapes=[pltpu.VMEM(dx.shape, BF16)],
        compiler_params=pltpu.CompilerParams(vmem_limit_bytes=8 * MIB),
        cost_estimate=pl.CostEstimate(flops=2 * slots * width * dx.shape[0], bytes_accessed=0, transcendentals=0),
        name="unpack",
    )(*args)


def local(x_stash, gain, w_in, w_out, out_grad, lengths, order):
    sections = lax.axis_size("section")
    replicas = lax.axis_size("dp")
    sel, xhat, rstd, u, hid, gp, top, gain_row, w_up, w_up_t, w_down, *stash = prep(
        lengths, order, x_stash[0], out_grad, gain, w_in[0], w_out[0])
    rows = u.shape[0] // CHUNKS
    swap = [(i, i ^ 1) for i in range(replicas)]
    arrived, got = {}, []
    half = sections // 2
    for section in reversed(range(sections)):
        hops = [(s, s - 1) for s in (section + half, section, section - half) if 0 < s < sections]
        for chunk in range(CHUNKS):
            if section == sections - 1 and chunk == 1:
                hid, gp = rest(u, w_up, hid, gp)
            stage = (top, xhat, rstd, gp, gain_row, w_up_t, w_down, u, hid)
            ship_rows = None
            if section == 0 and chunk >= CHUNKS - 2:
                ship_rows = (0, chunk * rows + rows) if chunk == CHUNKS - 2 else (chunk * rows, chunk * rows + rows)
            part = (chunk * rows, chunk * rows + rows)
            skip_dx = section == 0 and chunk == CHUNKS - 1
            *stash, = tick(section, part, arrived.get(chunk), stage, tuple(stash), ship_rows, skip_dx)
            if ship_rows:
                got.append(lax.ppermute(stash.pop(), "dp", swap))
            if section:
                arrived[chunk] = lax.ppermute(stash.pop(), "section", hops)
    da, dy, dx = stash
    grad_rows = unpack(part, sel, dx, dy, da, xhat, rstd, gain_row, w_up_t)
    grad_in, grad_out = reduce_grads(u, da, dy, hid, *got, grad_rows)
    return grad_rows[None], grad_in[None], grad_out[None]


def solution(mesh):
    return jax.shard_map(
        local,
        mesh=mesh,
        in_specs=(
            P("section", "dp", None),
            P("section", None),
            P("section", None, None),
            P("section", None, None),
            P("dp", None),
            P("dp", None),
            P("dp", None),
        ),
        out_specs=(P("section", "dp", None), P("section", "dp", None), P("section", "dp", None)),
        check_vma=False,
    )
```

```python
from functools import partial

import jax
import jax.numpy as jnp
from jax import lax
from jax.experimental import pallas as pl
from jax.experimental.pallas import tpu as pltpu
from jax.sharding import PartitionSpec as P

LIVE = 288
CHUNKS = 3
EPSILON = 1e-05
GELU_C = 0.7978845608028654
GELU_K = 0.044715
F32 = jnp.float32
BF16 = jnp.bfloat16

VMEM = pl.BlockSpec(memory_space=pltpu.VMEM)
HBM = pl.BlockSpec(memory_space=pltpu.HBM)
MIB = 1 << 20


def in_vmem(value):
    return pltpu.with_memory_space_constraint(value, pltpu.VMEM)


def vmem_array(shape, dtype):
    return pltpu.VMEM(shape, dtype)


def in_hbm(value):
    return pltpu.with_memory_space_constraint(value, pltpu.HBM)


def selector(len_ref, ord_ref, live, slots):
    count = len_ref.shape[1]
    width = slots // count
    p = lax.broadcasted_iota(jnp.int32, (live, slots), 0)
    q = lax.broadcasted_iota(jnp.int32, (live, slots), 1)
    target = jnp.full((live, slots), -1, jnp.int32)
    start = jnp.int32(0)
    for k in range(count):
        size = jnp.int32(0)
        for j in range(count):
            size = size + jnp.where(ord_ref[0, j] == k, len_ref[0, j], 0)
        inside = (q >= k * width) & (q < k * width + size)
        target = jnp.where(inside, q - k * width + start, target)
        start = start + size
    return (target == p).astype(F32).astype(BF16)


def gelu_rows(rows, cols, u_ref, w, hid_ref, gp_ref):
    a = jnp.dot(u_ref[rows, :], w, preferred_element_type=F32)
    square = a * a
    t = jnp.tanh(a * (GELU_C + (GELU_C * GELU_K) * square))
    half = 0.5 + 0.5 * t
    hid_ref[rows, cols] = (a * half).astype(BF16)
    slope = a * (0.5 * GELU_C + (1.5 * GELU_C * GELU_K) * square)
    gp_ref[rows, cols] = half + (1.0 - t * t) * slope


def prep_kernel(len_hbm, ord_hbm, x_hbm, og_hbm, gain_hbm, w_in_hbm, w_out_hbm,
                sel_ref, xhat_ref, rstd_ref, u_ref, hid_ref, gp_ref, top_ref, gain_ref, w_in_ref, w_in_t_ref, w_out_ref,
                da_ref, dy_ref, dx_ref, len_ref, ord_ref, x_ref, og_ref, sems):
    del da_ref, dy_ref, dx_ref
    block = 512
    blocks = [slice(i, i + block) for i in range(0, w_in_ref.shape[1], block)]
    pairs = [(len_hbm, len_ref), (ord_hbm, ord_ref), (x_hbm, x_ref), (gain_hbm, gain_ref)]
    pairs += [(w_in_hbm.at[:, cols], w_in_ref.at[:, cols]) for cols in blocks]
    pairs += [(og_hbm, og_ref), (w_out_hbm, w_out_ref)]
    copies = [pltpu.make_async_copy(source, target, sems.at[i]) for i, (source, target) in enumerate(pairs)]
    for copy in copies:
        copy.start()
    live, slots = sel_ref.shape
    copies[0].wait()
    copies[1].wait()
    sel = selector(len_ref, ord_ref, live, slots)
    sel_ref[...] = sel
    copies[2].wait()
    x = jnp.dot(sel, x_ref[...], preferred_element_type=F32)
    centre = x - jnp.mean(x, axis=1, keepdims=True)
    rstd = lax.rsqrt(jnp.mean(centre * centre, axis=1, keepdims=True) + EPSILON)
    xhat = centre * rstd
    xhat_ref[...] = xhat
    rstd_ref[...] = jnp.broadcast_to(rstd, rstd_ref.shape)
    copies[3].wait()
    u_ref[...] = (xhat * gain_ref[...]).astype(BF16)
    for copy, cols in zip(copies[4:-2], blocks):
        copy.wait()
        w = w_in_ref[:, cols]
        w_in_t_ref[cols, :] = w.T
        gelu_rows(slice(0, live // CHUNKS), cols, u_ref, w, hid_ref, gp_ref)
    copies[-2].wait()
    top_ref[...] = jnp.dot(sel, og_ref[...], preferred_element_type=F32).astype(BF16)
    copies[-1].wait()


def prep(lengths, order, x, out_grad, gain, w_in, w_out):
    slots, width = x.shape
    hidden = w_in.shape[1]
    live = LIVE * slots // 384
    args = (lengths, order, x, out_grad, gain, w_in, w_out)
    return pl.pallas_call(
        prep_kernel,
        out_shape=(
            vmem_array((live, slots), BF16),
            vmem_array((live, width), F32),
            vmem_array((live, 128), F32),
            vmem_array((live, width), BF16),
            vmem_array((live, hidden), BF16),
            vmem_array((live, hidden), F32),
            vmem_array((live, width), BF16),
            vmem_array(gain.shape, F32),
            vmem_array(w_in.shape, BF16),
            vmem_array((hidden, width), BF16),
            vmem_array(w_out.shape, BF16),
            vmem_array((live, hidden), BF16),
            vmem_array((live, width), BF16),
            vmem_array((live, width), BF16),
        ),
        in_specs=[HBM] * len(args),
        out_specs=(VMEM,) * 14,
        scratch_shapes=[
            pltpu.SMEM(lengths.shape, jnp.int32),
            pltpu.SMEM(order.shape, jnp.int32),
            pltpu.VMEM(x.shape, BF16),
            pltpu.VMEM(out_grad.shape, BF16),
            pltpu.SemaphoreType.DMA((len(args) - 1 + hidden // 512,)),
        ],
        compiler_params=pltpu.CompilerParams(vmem_limit_bytes=16 * MIB),
        cost_estimate=pl.CostEstimate(
            flops=2 * live * width * hidden, bytes_accessed=4 * width * hidden, transcendentals=live * hidden),
        name="prep",
    )(*(in_hbm(v) for v in args))


def rest_kernel(part, u_ref, w_in_ref, hid_in, gp_in, hid_ref, gp_ref):
    del hid_in, gp_in
    block = 512
    hidden = w_in_ref.shape[1]

    for i in range(hidden // block):
        cols = slice(i * block, (i + 1) * block)
        gelu_rows(slice(*part), cols, u_ref, w_in_ref[:, cols], hid_ref, gp_ref)


def rest(part, u, w_in, hid, gp):
    args = tuple(in_vmem(v) for v in (u, w_in, hid, gp))
    return pl.pallas_call(
        partial(rest_kernel, part),
        out_shape=(vmem_array(hid.shape, BF16), vmem_array(gp.shape, F32)),
        in_specs=[VMEM] * len(args),
        out_specs=(VMEM,) * 2,
        input_output_aliases={2: 0, 3: 1},
        compiler_params=pltpu.CompilerParams(vmem_limit_bytes=8 * MIB),
        cost_estimate=pl.CostEstimate(flops=2 * hid.size * u.shape[1], bytes_accessed=0, transcendentals=hid.size),
        name="rest",
    )(*args)


def tick_kernel(section, part, ship_rows, skip_dx, has_cur, *refs):
    cur_ref = refs[0] if has_cur else None
    (top_ref, xhat_ref, rstd_ref, gp_ref, gain_ref, w_in_t_ref, w_out_ref, u_ref, hid_ref,
     _, _, _, da_ref, dy_ref, dx_ref, *more) = refs[1:] if has_cur else refs
    hidden = w_in_t_ref.shape[0]
    width = w_out_ref.shape[0]
    rows = slice(*part)
    block = 512

    @pl.when(lax.axis_index("section") == section)
    def _():
        dy = cur_ref[...] if has_cur else top_ref[rows, :]
        dy_ref[rows, :] = dy
        for i in range(hidden // block):
            cols = slice(i * block, (i + 1) * block)
            dh = jnp.dot(dy, w_out_ref[:, cols], preferred_element_type=F32)
            da_ref[rows, cols] = (dh * gp_ref[rows, cols]).astype(BF16)
        if not skip_dx:
            dx = grad_rows_of(rows, dy, da_ref[rows, :], xhat_ref, rstd_ref, gain_ref, w_in_t_ref)
            dx_ref[rows, :] = dx
            if section:
                more[0][...] = dx

    if ship_rows:
        ship = more[-1]
        first = lax.rem(lax.axis_index("dp"), 2) == 0
        part = slice(*ship_rows)

        @pl.when(first)
        def _():
            ship[:, :width] = dy_ref[part, :]
            ship[:, width:] = hid_ref[part, :]

        @pl.when(jnp.logical_not(first))
        def _():
            ship[:, :width] = u_ref[part, :]
            ship[:, width:] = da_ref[part, :]


def tick(section, part, cur, stage, stash, ship_rows, skip_dx):
    live, hidden = stash[0].shape
    width = stash[1].shape[1]
    rows = part[1] - part[0]
    args = tuple(in_vmem(v) for v in (() if cur is None else (cur,)) + stage + stash)
    shapes = (
        vmem_array((live, hidden), BF16),
        vmem_array((live, width), BF16),
        vmem_array((live, width), BF16),
    )
    if section:
        shapes += (vmem_array((rows, width), BF16),)
    if ship_rows:
        shapes += (vmem_array((ship_rows[1] - ship_rows[0], width + hidden), BF16),)
    first = len(args) - len(stash)
    return pl.pallas_call(
        partial(tick_kernel, section, part, ship_rows, skip_dx, cur is not None),
        out_shape=shapes,
        in_specs=[VMEM] * len(args),
        out_specs=(VMEM,) * len(shapes),
        input_output_aliases={first + i: i for i in range(len(stash))},
        compiler_params=pltpu.CompilerParams(vmem_limit_bytes=8 * MIB),
        cost_estimate=pl.CostEstimate(
            flops=10 ** 10 if skip_dx else 4 * rows * width * hidden, bytes_accessed=0, transcendentals=0),
        name="tick",
    )(*args)


def ring_place(block):
    size = lax.axis_size("dp") // 2
    place = lax.axis_index("dp") // 2

    def rows(ahead, half):
        target = lax.rem(place + ahead + size, size)
        return pl.ds(pl.multiple_of(target * (2 * block) + half * block, 16), block)

    return rows


def stage_kernel(far, u_ref, da_ref, dy_ref, hid_ref, got_ref, lhs_ref, rhs_ref, right_ref, left_ref):
    live, width = u_ref.shape
    block = right_ref.shape[0]
    first = lax.rem(lax.axis_index("dp"), 2) == 0
    ready = live + got_ref.shape[0]

    @pl.when(first)
    def _():
        lhs_ref[:, :live] = u_ref[...].T
        rhs_ref[:live, :] = da_ref[...]

    @pl.when(jnp.logical_not(first))
    def _():
        lhs_ref[:, :live] = dy_ref[...].T
        rhs_ref[:live, :] = hid_ref[...]

    lhs_ref[:, live:ready] = got_ref[:, :width].T
    rhs_ref[live:ready, :] = got_ref[:, width:]
    rows = ring_place(block)
    right_ref[...] = jnp.dot(lhs_ref[rows(far, 0), :ready], rhs_ref[:ready, :], preferred_element_type=F32)
    left_ref[...] = jnp.dot(lhs_ref[rows(-far, 1), :ready], rhs_ref[:ready, :], preferred_element_type=F32)


def first_kernel(far, right_part, left_part, got_ref, lhs_in, rhs_in, right_ref, left_ref, lhs_ref, rhs_ref):
    del lhs_in, rhs_in
    width, rows_all = lhs_ref.shape
    block = right_ref.shape[0]
    ready = rows_all - got_ref.shape[0]
    lhs_ref[:, ready:] = got_ref[:, :width].T
    rhs_ref[ready:, :] = got_ref[:, width:]
    rows = ring_place(block)
    right = jnp.dot(lhs_ref[rows(far, 0), ready:], rhs_ref[ready:, :], preferred_element_type=F32)
    right_ref[...] = (right_part[...] + right).astype(BF16)
    left = jnp.dot(lhs_ref[rows(-far, 1), ready:], rhs_ref[ready:, :], preferred_element_type=F32)
    left_ref[...] = (left_part[...] + left).astype(BF16)


def second_kernel(far, lhs_ref, rhs_ref, right_ref, left_ref, next_right_ref, next_left_ref):
    rows = ring_place(right_ref.shape[0])
    right_ref[...] = jnp.dot(lhs_ref[rows(far - 1, 1), :], rhs_ref[...], preferred_element_type=F32).astype(BF16)
    left_ref[...] = jnp.dot(lhs_ref[rows(1 - far, 0), :], rhs_ref[...], preferred_element_type=F32).astype(BF16)
    next_right_ref[...] = jnp.dot(lhs_ref[rows(far - 1, 0), :], rhs_ref[...], preferred_element_type=F32)
    next_left_ref[...] = jnp.dot(lhs_ref[rows(1 - far, 1), :], rhs_ref[...], preferred_element_type=F32)


def near_kernel(reach, lhs_ref, rhs_ref, _, all_ref, near_ref):
    block = all_ref.shape[0] // (2 * (2 * reach + 1))
    rows = ring_place(block)
    for k in range(-reach, reach + 1):
        for half in range(2):
            at = (2 * (k + reach) + half) * block
            near_ref[at:at + block, :] = lhs_ref[rows(k, half), :]
    tile = 512
    for i in range(rhs_ref.shape[1] // tile):
        cols = slice(i * tile, (i + 1) * tile)
        all_ref[:, cols] = jnp.dot(near_ref[...], rhs_ref[:, cols], preferred_element_type=F32).astype(BF16)


def near_rows(all_ref, block, ahead, half):
    reach = (all_ref.shape[0] // (2 * block) - 1) // 2
    at = (2 * (ahead + reach) + half) * block
    return all_ref[at:at + block, :].astype(F32)


def early_hop_kernel(own_right_ref, own_left_ref, from_left_ref, from_right_ref, right_ref, left_ref):
    right_ref[...] = (from_left_ref[...].astype(F32) + own_right_ref[...]).astype(BF16)
    left_ref[...] = (from_right_ref[...].astype(F32) + own_left_ref[...]).astype(BF16)


def hop_kernel(ahead, half, all_ref, from_left_ref, from_right_ref, *refs):
    right_ref, left_ref = refs[-2:]
    block = right_ref.shape[0]
    right_ref[...] = (from_left_ref[...].astype(F32) + near_rows(all_ref, block, ahead, half)).astype(BF16)
    left_ref[...] = (from_right_ref[...].astype(F32) + near_rows(all_ref, block, -ahead, 1 - half)).astype(BF16)


def last_kernel(all_ref, right_0, left_1, right_1, left_0, keep_ref, send_ref):
    block = keep_ref.shape[0]
    first = lax.rem(lax.axis_index("dp"), 2) == 0
    half_0 = right_0[...].astype(F32) + left_0[...].astype(F32) + near_rows(all_ref, block, 0, 0)
    half_1 = right_1[...].astype(F32) + left_1[...].astype(F32) + near_rows(all_ref, block, 0, 1)
    scale = 1.0 / lax.axis_size("dp")
    keep_ref[...] = jnp.where(first, half_0, half_1) * scale
    send_ref[...] = jnp.where(first, half_1, half_0).astype(BF16)


def output_kernel(keep_ref, got_ref, in_ref, out_ref):
    first = lax.rem(lax.axis_index("dp"), 2) == 0
    got = got_ref[...].astype(F32) * (1.0 / lax.axis_size("dp"))
    keep = keep_ref[...]
    in_ref[...] = jnp.where(first, keep, got)
    out_ref[...] = jnp.where(first, got, keep)


def kernel_call(body, shapes, args, flops, name, aliases=None, gate=None, scratch=()):
    specs = [VMEM] * len(args)
    args = tuple(in_vmem(v) for v in args)
    if gate is not None:
        specs.append(HBM)
        args += (in_hbm(gate),)
    return pl.pallas_call(
        body,
        out_shape=shapes,
        in_specs=specs,
        out_specs=(VMEM,) * len(shapes),
        scratch_shapes=scratch,
        input_output_aliases=aliases or {},
        compiler_params=pltpu.CompilerParams(vmem_limit_bytes=8 * MIB),
        cost_estimate=pl.CostEstimate(flops=flops, bytes_accessed=0, transcendentals=0),
        name=name,
    )(*args)


def reduce_grads(u, da, dy, hid, got_a, got_b, gate):
    live, width = u.shape
    hidden = da.shape[1]
    count = lax.axis_size("dp")
    far = count // 4
    block = width // count
    piece = vmem_array((block, hidden), BF16)
    wide = vmem_array((block, hidden), F32)
    lhs_shape, rhs_shape = vmem_array((width, 2 * live), BF16), vmem_array((2 * live, hidden), BF16)
    small = 8 * block * live * hidden

    def around(value, chips):
        return lax.ppermute(value, "dp", [(i, (i + 2 * chips) % count) for i in range(count)])

    lhs, rhs, right, left = kernel_call(
        partial(stage_kernel, far), (lhs_shape, rhs_shape, wide, wide), (u, da, dy, hid, got_a), small, "stage")
    right, left, lhs, rhs = kernel_call(
        partial(first_kernel, far), (piece, piece, lhs_shape, rhs_shape), (right, left, got_b, lhs, rhs), small,
        "first_blocks", {3: 2, 4: 3})
    even = around(right, 1), around(left, -1)
    right, left, *own = kernel_call(
        partial(second_kernel, far), (piece, piece, wide, wide), (lhs, rhs), small, "second_blocks")
    odd = around(right, 1), around(left, -1)
    right, left = kernel_call(early_hop_kernel, (piece, piece), (*own, *even), 10 ** 9, "early_hop")
    even = around(right, 1), around(left, -1)
    near = (2 * far - 3) * 2 * block
    (total,) = kernel_call(
        partial(near_kernel, far - 2), (vmem_array((near, hidden), BF16),), (lhs, rhs, right),
        4 * near * live * hidden, "near_blocks", scratch=[pltpu.VMEM((near, 2 * live), BF16)])
    for ahead in range(far - 2, 0, -1):
        right, left = kernel_call(
            partial(hop_kernel, ahead, 1), (piece, piece), (total,) + odd, 10 ** 9, "hop_odd")
        odd = around(right, 1), around(left, -1)
        right, left = kernel_call(
            partial(hop_kernel, ahead, 0), (piece, piece), (total,) + even, 10 ** 9, "hop_even",
            gate=gate if ahead == 1 else None)
        even = around(right, 1), around(left, -1)
    keep, send = kernel_call(last_kernel, (wide, piece), (total,) + even + odd, 10 ** 9, "last_sum")
    got = lax.ppermute(send, "dp", [(i, i ^ 1) for i in range(count)])
    return kernel_call(
        output_kernel, (jax.ShapeDtypeStruct((block, hidden), F32),) * 2, (keep, got), 10 ** 8, "outputs")


def grad_rows_of(rows, dy, da, xhat_ref, rstd_ref, gain_ref, w_in_t_ref):
    g = jnp.concatenate(
        [jnp.dot(da, w_in_t_ref[:, i:i + 256], preferred_element_type=F32) for i in range(0, dy.shape[1], 256)], axis=1)
    g = g * gain_ref[...]
    xhat = xhat_ref[rows, :]
    inner = g - jnp.mean(g, axis=1, keepdims=True) - xhat * jnp.mean(g * xhat, axis=1, keepdims=True)
    return (dy.astype(F32) + rstd_ref[rows, 0:1] * inner).astype(BF16)


def unpack_kernel(part, sel_ref, dx_ref, dy_ref, da_ref, xhat_ref, rstd_ref, gain_ref, w_in_t_ref, out_ref, rows_ref):
    rows = slice(*part)
    rows_ref[...] = dx_ref[...]

    @pl.when(lax.axis_index("section") == 0)
    def _():
        rows_ref[rows, :] = grad_rows_of(rows, dy_ref[rows, :], da_ref[rows, :], xhat_ref, rstd_ref, gain_ref, w_in_t_ref)

    out_ref[...] = lax.dot_general(
        sel_ref[...], rows_ref[...], (((0,), (0,)), ((), ())), preferred_element_type=F32).astype(BF16)


def unpack(part, sel, dx, *rest_args):
    slots, width = sel.shape[1], dx.shape[1]
    args = tuple(in_vmem(v) for v in (sel, dx) + rest_args)
    return pl.pallas_call(
        partial(unpack_kernel, part),
        out_shape=jax.ShapeDtypeStruct((slots, width), BF16),
        in_specs=[VMEM] * len(args),
        out_specs=VMEM,
        scratch_shapes=[pltpu.VMEM(dx.shape, BF16)],
        compiler_params=pltpu.CompilerParams(vmem_limit_bytes=8 * MIB),
        cost_estimate=pl.CostEstimate(flops=2 * slots * width * dx.shape[0], bytes_accessed=0, transcendentals=0),
        name="unpack",
    )(*args)


def local(x_stash, gain, w_in, w_out, out_grad, lengths, order):
    sections = lax.axis_size("section")
    replicas = lax.axis_size("dp")
    sel, xhat, rstd, u, hid, gp, top, gain_row, w_up, w_up_t, w_down, *stash = prep(
        lengths, order, x_stash[0], out_grad, gain, w_in[0], w_out[0])
    rows = u.shape[0] // CHUNKS
    swap = [(i, i ^ 1) for i in range(replicas)]
    arrived, got = {}, []
    half = sections // 2
    for section in reversed(range(sections)):
        hops = [(s, s - 1) for s in (section + half, section, section - half) if 0 < s < sections]
        for chunk in range(CHUNKS):
            part = (chunk * rows, chunk * rows + rows)
            if section == sections - 1 and chunk:
                hid, gp = rest(part, u, w_up, hid, gp)
            stage = (top, xhat, rstd, gp, gain_row, w_up_t, w_down, u, hid)
            ship_rows = None
            if section == 0 and chunk >= CHUNKS - 2:
                ship_rows = (0, chunk * rows + rows) if chunk == CHUNKS - 2 else (chunk * rows, chunk * rows + rows)
            skip_dx = section == 0 and chunk == CHUNKS - 1
            *stash, = tick(section, part, arrived.get(chunk), stage, tuple(stash), ship_rows, skip_dx)
            if ship_rows:
                got.append(lax.ppermute(stash.pop(), "dp", swap))
            if section:
                arrived[chunk] = lax.ppermute(stash.pop(), "section", hops)
    da, dy, dx = stash
    grad_rows = unpack(part, sel, dx, dy, da, xhat, rstd, gain_row, w_up_t)
    grad_in, grad_out = reduce_grads(u, da, dy, hid, *got, grad_rows)
    return grad_rows[None], grad_in[None], grad_out[None]


def solution(mesh):
    return jax.shard_map(
        local,
        mesh=mesh,
        in_specs=(
            P("section", "dp", None),
            P("section", None),
            P("section", None, None),
            P("section", None, None),
            P("dp", None),
            P("dp", None),
            P("dp", None),
        ),
        out_specs=(P("section", "dp", None), P("section", "dp", None), P("section", "dp", None)),
        check_vma=False,
    )
```
